32 devices in a mesh: groups: 2 (over y), patch: 4 (over z), chan: 2 (over x), sub: 2 (over core).
Axes of the slice: x: 2, y: 2, z: 4, core: 2. Of those that a mesh axis runs over, the one named last changes fastest.
Arguments:
- latent: bfloat16 [640, 2048], P(('chan', 'sub'), ('groups', 'patch')), parts along dimension 1, may hold values from -18 to 18
- timestep: int32 [2], P('groups'), parts along dimension 0, may hold values from 0 to 999
- time_w1: bfloat16 [1280, 320], replicated, may hold values from -0.3125 to 0.3125
- time_proj: bfloat16 [640, 1280], P(('chan', 'sub')), may hold values from -0.15625 to 0.15625
- conv1_w: bfloat16 [9, 640, 640], P(None, ('chan', 'sub')), may hold values from -0.078125 to 0.078125
- conv2_w: bfloat16 [9, 640, 640], P(None, ('chan', 'sub')), may hold values from -0.078125 to 0.078125
- proj_in_w: bfloat16 [640, 640], P(('chan', 'sub')), may hold values from -0.25 to 0.25
- q_w: bfloat16 [640, 640], P(('chan', 'sub')), may hold values from -8 to 8
- kv_w: bfloat16 [2, 640, 640], P(None, ('chan', 'sub')), may hold values from -8 to 8
- out_w: bfloat16 [640, 640], P(('chan', 'sub')), may hold values from -0.25 to 0.25
- proj_out_w: bfloat16 [640, 640], P(('chan', 'sub')), may hold values from -0.25 to 0.25
Outputs:
- output: bfloat16 [640, 2048], P(('chan', 'sub'), ('groups', 'patch')), parts along dimension 1
The draws below stay inside these ranges and needn't reach their ends.
There are 2 independent parts, one for each index of `groups`. The reference program is written for one: setup_inputs(seed, part) draws one part's arguments, and reference() takes and returns one part's arrays. A program takes and returns all parts, laid end to end along the dimension named above; an argument that names none is the same for every part. Nothing has to cross between parts.
All inputs are finite; a program needn't handle non-finite values.
Results may differ from the reference program's by a relative error of at most 0.02.
Values may be sent and summed in bfloat16 or wider, within the bound.
A program may use at most 64 MiB of HBM per device.

```python
import math
import jax
import jax.numpy as jnp
from jax import lax

C = 640
HEADS = 10
HEAD_DIM = 64
NGROUPS = 32
TEMB = 1280
FREQ = 320
WIDTH = 256
TOKENS = 1024


def draw_latent(key, part):
    height = TOKENS // WIDTH
    subkeys = jax.random.split(key, 4)
    row_index = (jnp.arange(TOKENS) // WIDTH).astype(jnp.float32)
    row_slope = row_index / max(height - 1, 1)
    base_noise = jnp.clip(jax.random.normal(subkeys[0], (C, TOKENS), jnp.float32), -4.0, 4.0)
    log_level = 0.5 * row_slope + 0.5 * jax.random.uniform(subkeys[1], (TOKENS,), jnp.float32)
    token_scale = 0.3 * jnp.exp(math.log(10.0) * log_level)
    channel_scale = jnp.exp(jax.random.uniform(subkeys[3], (C, 1), jnp.float32, math.log(0.7), math.log(1.4)))
    latent_field = base_noise * token_scale[None, :] * channel_scale
    return latent_field.astype(jnp.bfloat16)


def attention_weights(key):
    subkeys = jax.random.split(jax.random.fold_in(key, 101), 4)
    scale = C ** (-0.5)
    query_w = jnp.clip(jax.random.normal(subkeys[0], (C, C), jnp.float32), -4.0, 4.0) * (1.6 * scale)
    key_w = jnp.clip(jax.random.normal(subkeys[2], (C, C), jnp.float32), -4.0, 4.0) * (1.6 * scale)
    value_w = jnp.clip(jax.random.normal(subkeys[3], (C, C), jnp.float32), -4.0, 4.0) * (3.0 * scale)
    return (query_w, jnp.stack([key_w, value_w]))


def draw_q_w(key, part):
    return attention_weights(key)[0].astype(jnp.bfloat16)


def draw_kv_w(key, part):
    return attention_weights(key)[1].astype(jnp.bfloat16)


def level_of(key, dims, cuts, least, high):
    gain, own = 1.0, jax.random.fold_in(key, 6)
    for position, parts in cuts:
        steps = jnp.exp(jax.random.uniform(jax.random.fold_in(own, position), (parts,), jnp.float32, least / len(cuts), high / len(cuts)))
        gain = gain * jnp.repeat(steps, dims[position] // parts).reshape([-1 if axis == position else 1 for axis in range(len(dims))])
    return gain


def scatter_about(stream_key, extent, width, reach, cuts=(), kind=jnp.bfloat16):
    array = jax.random.normal(stream_key, extent, jnp.float32) * width
    if len(cuts) > 0:
        array = level_of(stream_key, extent, cuts, -0.22, 0.18) * array
    return jnp.clip(array, min=-reach, max=reach).astype(kind)


def setup_inputs(seed: int = 0, part: int = 0) -> dict:
    key_of = jax.random.split(jax.random.key(seed), 12)
    part_splits = jax.random.split(jax.random.fold_in(key_of[11], part), 12)
    return {
        "latent": draw_latent(jax.random.fold_in(jax.random.fold_in(key_of[11], part), 71), part),
        "timestep": jax.random.randint(part_splits[1], (1,), 0, 1000).astype(jnp.int32),
        "time_w1": scatter_about(key_of[2], (TEMB, FREQ), FREQ ** -0.5, 0.3125),
        "time_proj": scatter_about(key_of[3], (C, TEMB), TEMB ** -0.5, 0.15625, ((0, 4),)),
        "conv1_w": scatter_about(key_of[4], (9, C, C), (9 * C) ** -0.5, 0.078125, ((1, 4),)),
        "conv2_w": scatter_about(key_of[5], (9, C, C), (9 * C) ** -0.5, 0.078125, ((1, 4),)),
        "proj_in_w": scatter_about(key_of[6], (C, C), C ** -0.5, 0.25, ((0, 4),)),
        "q_w": draw_q_w(jax.random.fold_in(key_of[11], 71), part),
        "kv_w": draw_kv_w(jax.random.fold_in(key_of[11], 71), part),
        "out_w": scatter_about(key_of[9], (C, C), C ** -0.5, 0.25, ((0, 4),)),
        "proj_out_w": scatter_about(key_of[10], (C, C), C ** -0.5, 0.25, ((0, 4),)),
    }


def rounded(values):
    return lax.optimization_barrier(values.astype(jnp.bfloat16)).astype(jnp.float32)

def group_norm(values, epsilon):
    grouped = values.reshape(NGROUPS, C // NGROUPS, -1)
    centre = lax.optimization_barrier(jnp.mean(grouped, axis=(1, 2), keepdims=True))
    spread = lax.optimization_barrier(jnp.mean((grouped - centre) * (grouped - centre), axis=(1, 2), keepdims=True))
    return ((grouped - centre) / jnp.sqrt(spread + epsilon)).reshape(C, -1)

def convolve(active, weight):
    height = TOKENS // WIDTH
    padded = jnp.pad(active.reshape(C, height, WIDTH), ((0, 0), (1, 1), (1, 1)))
    running = jnp.zeros((C, TOKENS), jnp.float32)
    for offset in range(9):
        row_step, col_step = divmod(offset, 3)
        window = padded[:, row_step:row_step + height, col_step:col_step + WIDTH].reshape(C, TOKENS)
        running = running + jnp.dot(weight[offset], window, preferred_element_type=jnp.float32)
    return running

def time_bias_of(timestep, time_w1, time_proj):
    half_width = FREQ // 2
    frequency = jnp.exp(-math.log(10000.0) * jnp.arange(half_width, dtype=jnp.float32) / half_width)
    angles = timestep[0].astype(jnp.float32) * frequency
    embedded = jnp.concatenate([jnp.cos(angles), jnp.sin(angles)]).astype(jnp.bfloat16)
    hidden = jax.nn.silu(jnp.dot(time_w1, embedded, preferred_element_type=jnp.float32))
    return jnp.dot(time_proj, jax.nn.silu(hidden).astype(jnp.bfloat16), preferred_element_type=jnp.float32)

def attention(layer_normed, q_w, kv_w):
    queries = jnp.dot(q_w, layer_normed, preferred_element_type=jnp.float32) * 0.125
    key_heads = rounded(jnp.dot(kv_w[0], layer_normed, preferred_element_type=jnp.float32)).reshape(HEADS, HEAD_DIM, TOKENS)
    value_heads = rounded(jnp.dot(kv_w[1], layer_normed, preferred_element_type=jnp.float32)).reshape(HEADS, HEAD_DIM, TOKENS)
    block_size = math.gcd(TOKENS, 512)
    block_count = TOKENS // block_size
    query_blocks = rounded(queries).reshape(HEADS, HEAD_DIM, block_count, block_size).transpose(2, 0, 1, 3)

    def one_block(query_block):
        scores = jnp.einsum('hdk,hdb->hkb', key_heads, query_block, precision=lax.Precision.HIGHEST)
        row_peak = lax.optimization_barrier(jnp.max(scores, axis=1, keepdims=True))
        weights = jnp.exp(scores - row_peak)
        row_total = lax.optimization_barrier(jnp.sum(weights, axis=1))
        weighted = jnp.einsum('hdk,hkb->hdb', value_heads, rounded(weights), precision=lax.Precision.HIGHEST)
        return (weighted / row_total[:, None, :]).astype(jnp.bfloat16)
    blocks = lax.map(one_block, query_blocks)
    return blocks.transpose(1, 2, 0, 3).reshape(C, TOKENS)

def reference(latent, timestep, time_w1, time_proj, conv1_w, conv2_w, proj_in_w, q_w, kv_w, out_w, proj_out_w):
    latent_f32 = latent.astype(jnp.float32)
    time_bias = time_bias_of(timestep, time_w1, time_proj)
    act_one = jax.nn.silu(group_norm(latent_f32, 1e-05)).astype(jnp.bfloat16)
    conv_one = (convolve(act_one, conv1_w) + time_bias[:, None]).astype(jnp.bfloat16)
    act_two = jax.nn.silu(group_norm(conv_one.astype(jnp.float32), 1e-05)).astype(jnp.bfloat16)
    resnet = (latent_f32 + convolve(act_two, conv2_w)).astype(jnp.bfloat16)
    normed = group_norm(resnet.astype(jnp.float32), 1e-06).astype(jnp.bfloat16)
    projected = jnp.dot(proj_in_w, normed, preferred_element_type=jnp.float32).astype(jnp.bfloat16)
    proj_f32 = projected.astype(jnp.float32)
    centre = lax.optimization_barrier(jnp.mean(proj_f32, axis=0, keepdims=True))
    spread = lax.optimization_barrier(jnp.mean((proj_f32 - centre) * (proj_f32 - centre), axis=0, keepdims=True))
    layer_normed = ((proj_f32 - centre) / jnp.sqrt(spread + 1e-05)).astype(jnp.bfloat16)
    attended = attention(layer_normed, q_w, kv_w)
    mixed = (proj_f32 + jnp.dot(out_w, attended, preferred_element_type=jnp.float32)).astype(jnp.bfloat16)
    return (resnet.astype(jnp.float32) + jnp.dot(proj_out_w, mixed, preferred_element_type=jnp.float32)).astype(jnp.bfloat16)
```

```python
import functools
import math

import jax
import jax.numpy as jnp
from jax import lax
from jax.experimental import pallas as pl
from jax.experimental.pallas import tpu as pltpu
from jax.sharding import PartitionSpec as P

C = 640
HEADS = 10
HEAD_DIM = 64
NGROUPS = 32
FREQ = 320
WIDTH = 256
GROUP = C // NGROUPS
MESH = pl.DeviceIdType.MESH
F32 = jnp.float32
BF16 = jnp.bfloat16
HIGH = lax.Precision.HIGHEST

G_PW, G_OW, G_Q, G_K, G_V, G_X1, G_X2, G_X3, G_AT, G_S1, G_S2, G_S3 = range(12)
G_LN = 12


def dot(a, b, precision=None):
    return jnp.dot(a, b, preferred_element_type=F32, precision=precision)


def dot_nt(a, b):
    return lax.dot_general(a, b, (((1,), (1,)), ((), ())), preferred_element_type=F32)


def dot_tn(a, b):
    return lax.dot_general(a, b, (((0,), (0,)), ((), ())), preferred_element_type=F32)


def loop(low, high, body):
    if high - low <= 4:
        for k in range(low, high):
            body(k)
    else:
        lax.fori_loop(low, high, lambda k, _: (body(k), 0)[1], 0)


def silu(v):
    return v / (1.0 + jnp.exp(-v))


def kernel(
    npatch, nchan, nsub, own, nheads,
    latent, emb, time_w1, time_proj, conv1_w, conv2_w, proj_in_w, q_w, kv_w, out_w, proj_out_w,
    out,
    tw1, tpj, cw1, cw2, po, pw, ow, qw, kw, vw, x1, x2, x3, at, zst, cst, hsend, hrecv,
    ln, vals, scores, attn, proj, res,
    lsem, gsend, grecv, zsend, zrecv, hssem, hrsem, lnsend, lnrecv,
):
    band = lax.axis_index("patch")
    chan = lax.axis_index("chan")
    sub = lax.axis_index("sub")
    idx = chan * nsub + sub
    nidx = nchan * nsub
    tokens = latent.shape[1]
    aligned = (own * nsub) % HEAD_DIM == 0

    def rows(block, size):
        return pl.ds(pl.multiple_of(block * size, size if size == 8 else 16), size)

    mine = rows(idx, own)
    pairs = [
        (conv1_w, cw1), (time_w1, tw1), (time_proj, tpj), (q_w, qw.at[mine]),
        (kv_w.at[0], kw.at[mine]), (kv_w.at[1], vw.at[mine]), (proj_in_w, pw.at[mine]),
        (conv2_w, cw2), (out_w, ow.at[mine]), (proj_out_w, po),
    ]
    loads = [pltpu.make_async_copy(a, b, lsem.at[i]) for i, (a, b) in enumerate(pairs)]
    L_C1, L_T1, L_TP, L_Q, L_K, L_V, L_PW, L_C2, L_OW, L_PO = loads
    for load in loads:
        load.start()

    def other(k, by, count):
        return lax.rem(k + by + count, count)

    class Gather:
        def __init__(self, g, buf, size, only_sub=False):
            self.g, self.buf, self.size = g, buf, size
            self.chans = 1 if only_sub else nchan

        def copy(self, block, d, s):
            ref = self.buf.at[rows(block, self.size)]
            to = {"chan": other(chan, d, nchan)} if s == 0 else {"sub": other(sub, s, nsub)}
            return pltpu.make_async_remote_copy(
                src_ref=ref, dst_ref=ref, send_sem=gsend.at[self.g, d, s],
                recv_sem=grecv.at[self.g, d, s], device_id=to, device_id_type=MESH,
            )

        def start(self):
            for d in range(1, self.chans):
                self.copy(idx, d, 0).start()
            for s in range(1, nsub):
                self.copy(idx, 0, s).start()

        def forward(self):
            for d in range(1, self.chans):
                block = other(chan, -d, nchan) * nsub + sub
                self.copy(block, d, 0).wait_recv()
                for s in range(1, nsub):
                    self.copy(block, d, s).start()

        def finish(self):
            for d in range(self.chans):
                for s in range(1, nsub):
                    block = other(chan, -d, nchan) * nsub + other(sub, -s, nsub)
                    self.copy(block, d, s).wait_recv()

        def drain(self):
            for d in range(self.chans):
                for s in range(nsub):
                    if d or s:
                        self.copy(idx, d, s).wait_send()

    gw = [
        Gather(G_Q, qw, own, aligned), Gather(G_K, kw, own, aligned), Gather(G_V, vw, own, aligned),
    ]
    gpw, gow = Gather(G_PW, pw, own), Gather(G_OW, ow, own)
    gx = [Gather(G_X1, x1, own), Gather(G_X2, x2, own), Gather(G_X3, x3, own)]
    gat = Gather(G_AT, at, own)
    gst = [Gather(G_S1 + i, cst.at[i], 8) for i in range(3)]

    cell = GROUP * tokens

    def members(shape, group_dim, size):
        gi = lax.broadcasted_iota(jnp.int32, shape, group_dim)
        ci = lax.broadcasted_iota(jnp.int32, shape, 1 - group_dim)
        g = gi & 7
        first = (gi >> 3) * size + g * GROUP
        inside = (ci >= first) & (ci < first + GROUP) & (g < size // GROUP)
        return jnp.where(inside, 1.0, 0.0).astype(F32)

    def stats(x, layer):
        e = members((8, own), 0, own)
        et = members((own, 8), 1, own)
        mean = jnp.sum(dot(e, x, HIGH), axis=1, keepdims=True) * (1.0 / cell)
        mean = jnp.broadcast_to(mean, (8, 128))
        mc = dot(et, mean, HIGH)
        dev = x - jnp.concatenate([mc] * (tokens // 128), axis=1)
        m2 = jnp.sum(dot(e, dev * dev, HIGH), axis=1, keepdims=True)
        lane = lax.broadcasted_iota(jnp.int32, (8, 128), 1)
        zst[layer, band] = jnp.where(lane < 64, mean, m2)

    def zcopy(layer, o):
        ref = zst.at[layer, band]
        return pltpu.make_async_remote_copy(
            src_ref=ref, dst_ref=ref, send_sem=zsend.at[layer, o], recv_sem=zrecv.at[layer, o],
            device_id={"patch": other(band, o, npatch)}, device_id_type=MESH,
        )

    def zarrived(layer, o):
        ref = zst.at[layer, other(band, -o, npatch)]
        pltpu.make_async_remote_copy(
            src_ref=ref, dst_ref=ref, send_sem=zsend.at[layer, o], recv_sem=zrecv.at[layer, o],
            device_id={"patch": other(band, o, npatch)}, device_id_type=MESH,
        ).wait_recv()

    def combined(layer, eps):
        loop(1, npatch, lambda o: zarrived(layer, o))
        tile = zst[layer]
        means, m2s = tile[:, :, 0:1], tile[:, :, 127:128]
        mean = jnp.sum(means, axis=0) * (1.0 / npatch)
        dev = means - mean[None]
        var = jnp.sum(m2s + cell * (dev * dev), axis=0) * (1.0 / (cell * npatch))
        lane = lax.broadcasted_iota(jnp.int32, (8, 128), 1)
        cst[layer, rows(idx, 8)] = jnp.where(
            lane < 64, jnp.broadcast_to(mean, (8, 128)),
            jnp.broadcast_to(lax.rsqrt(var + eps), (8, 128)),
        )
        gst[layer].start()

    def normalize(x, layer):
        both = dot(members((C, nidx * 8), 1, own), cst[layer], HIGH)
        return (x.astype(F32) - both[:, 0:1]) * both[:, 64:65]

    def hcopy(layer, way):
        return pltpu.make_async_remote_copy(
            src_ref=hsend.at[layer, way], dst_ref=hrecv.at[layer, way],
            send_sem=hssem.at[layer, way], recv_sem=hrsem.at[layer, way],
            device_id={"patch": other(band, 1 - 2 * way, npatch)}, device_id_type=MESH,
        )

    has_above, has_below = band > 0, band < npatch - 1

    def convolve(act, weight, layer):
        col = lax.broadcasted_iota(jnp.int32, act.shape, 1)
        taps = [
            jnp.where(col == 0, 0.0, pltpu.roll(act, 1, 1)).astype(BF16),
            act.astype(BF16),
            jnp.where(col == tokens - 1, 0.0, pltpu.roll(act, tokens - 1, 1)).astype(BF16),
        ]

        def row(i):
            return sum(dot(weight[3 * i + j], taps[j]) for j in range(3))

        hsend[layer, 0] = row(0).astype(BF16)

        @pl.when(has_below)
        def _():
            hcopy(layer, 0).start()

        hsend[layer, 1] = row(2).astype(BF16)

        @pl.when(has_above)
        def _():
            hcopy(layer, 1).start()

        return row(1)

    def neighbours(layer):
        @pl.when(has_above)
        def _():
            hcopy(layer, 0).wait_recv()

        @pl.when(has_below)
        def _():
            hcopy(layer, 1).wait_recv()

        return hrecv[layer, 0].astype(F32) + hrecv[layer, 1].astype(F32)

    for layer in range(2):
        @pl.when(jnp.logical_not(has_above))
        def _():
            hrecv[layer, 0] = jnp.zeros((own, tokens), BF16)

        @pl.when(jnp.logical_not(has_below))
        def _():
            hrecv[layer, 1] = jnp.zeros((own, tokens), BF16)

    x1[mine, :] = latent[...]
    lat = latent[...].astype(F32)
    stats(lat, 0)

    barrier = pltpu.get_barrier_semaphore()
    for d in range(1, nchan):
        pl.semaphore_signal(barrier, inc=1, device_id={"chan": other(chan, d, nchan)}, device_id_type=MESH)
    for s in range(1, nsub):
        pl.semaphore_signal(barrier, inc=1, device_id={"sub": other(sub, s, nsub)}, device_id_type=MESH)
    loop(1, npatch, lambda o: pl.semaphore_signal(
        barrier, inc=1, device_id={"patch": other(band, o, npatch)}, device_id_type=MESH))
    pl.semaphore_wait(barrier, nchan + nsub + npatch - 3)

    loop(1, npatch, lambda o: zcopy(0, o).start())
    gx[0].start()
    L_T1.wait()
    hidden = silu(dot_nt(emb[...], tw1[...]))
    L_TP.wait()
    bias = dot_nt(tpj[...], silu(hidden).astype(BF16))
    gx[0].forward()
    combined(0, 1e-05)
    gst[0].forward()
    for load, g in zip((L_Q, L_K, L_V), gw):
        load.wait()
        g.start()
    gx[0].finish()
    gst[0].finish()
    L_PW.wait()
    gpw.start()
    L_C1.wait()
    centre = convolve(silu(normalize(x1[...], 0)), cw1, 0)
    conv_one = (centre + neighbours(0) + jnp.concatenate([bias] * (tokens // 128), axis=1)).astype(BF16)
    x2[mine, :] = conv_one
    stats(conv_one.astype(F32), 1)

    loop(1, npatch, lambda o: zcopy(1, o).start())
    gx[1].start()
    gpw.forward()
    gx[1].forward()
    combined(1, 1e-05)
    gst[1].forward()
    gx[1].finish()
    gst[1].finish()
    L_OW.wait()
    gow.start()
    L_C2.wait()
    centre = convolve(silu(normalize(x2[...], 1)), cw2, 1)
    resnet = (lat + (centre + neighbours(1))).astype(BF16)
    res[...] = resnet
    x3[mine, :] = resnet
    stats(resnet.astype(F32), 2)

    loop(1, npatch, lambda o: zcopy(2, o).start())
    gx[2].start()
    gow.forward()
    gx[2].forward()
    combined(2, 1e-06)
    gst[2].forward()
    gpw.finish()
    gx[2].finish()
    gst[2].finish()
    projected = dot(pw[...], normalize(x3[...], 2).astype(BF16)).astype(BF16)
    proj[...] = projected
    wide = projected.astype(F32)
    wide = wide - jnp.mean(wide, axis=0, keepdims=True)
    spread = jnp.mean(wide * wide, axis=0, keepdims=True)
    ln[band] = (wide * lax.rsqrt(spread + 1e-05)).astype(BF16)

    def lncopy(o, source):
        ref = ln.at[source, mine]
        return pltpu.make_async_remote_copy(
            src_ref=ref, dst_ref=ref, send_sem=lnsend.at[o], recv_sem=lnrecv.at[o],
            device_id={"patch": other(band, o, npatch)}, device_id_type=MESH,
        )

    def gln(o):
        return Gather(G_LN + o, ln.at[other(band, -o, npatch)], own)

    loop(1, npatch, lambda o: lncopy(o, band).start())
    for g in gw:
        if not aligned:
            g.forward()
        g.finish()

    head0 = (idx * own) // HEAD_DIM
    span = nheads * HEAD_DIM
    held = pl.ds(pl.multiple_of(head0 * HEAD_DIM, HEAD_DIM), span)
    query = (dot(qw[held, :], ln[band]) * 0.125).astype(BF16)

    def score(source):
        tokens_of = ln[source]
        keys = dot(kw[held, :], tokens_of).astype(BF16)
        vals[source] = dot(vw[held, :], tokens_of).astype(BF16)
        for h in range(nheads):
            part = slice(h * HEAD_DIM, (h + 1) * HEAD_DIM)
            scores[source, h] = dot_tn(keys[part], query[part])

    def relay(o):
        lncopy(o, other(band, -o, npatch)).wait_recv()
        gln(o).start()

    score(band)
    loop(1, npatch, relay)
    loop(1, npatch, lambda o: gln(o).forward())

    def arrive(o):
        gln(o).finish()
        score(other(band, -o, npatch))

    loop(1, npatch, arrive)

    for h in range(nheads):
        part = slice(h * HEAD_DIM, (h + 1) * HEAD_DIM)

        def peak_of(b, peak):
            return jnp.maximum(peak, jnp.max(scores[b, h], axis=0, keepdims=True))

        def add(b, so_far):
            total, weighted = so_far
            weights = jnp.exp(scores[b, h] - peak)
            total = total + jnp.sum(weights, axis=0, keepdims=True)
            return total, weighted + dot(vals[b, part], weights.astype(BF16))

        peak = jnp.full((1, tokens), -jnp.inf, F32)
        so_far = (jnp.zeros((1, tokens), F32), jnp.zeros((HEAD_DIM, tokens), F32))
        if npatch <= 4:
            for b in range(npatch):
                peak = peak_of(b, peak)
            for b in range(npatch):
                so_far = add(b, so_far)
        else:
            peak = lax.fori_loop(0, npatch, peak_of, peak)
            so_far = lax.fori_loop(0, npatch, add, so_far)
        attn[part, :] = (so_far[1] / so_far[0]).astype(BF16)

    skip = pl.multiple_of(idx * own - head0 * HEAD_DIM, 16)
    at[mine, :] = attn[pl.ds(skip, own), :]
    gat.start()
    gat.forward()
    gow.finish()
    gat.finish()
    mixed = (proj[...].astype(F32) + dot(ow[...], at[...])).astype(BF16)
    L_PO.wait()
    out[...] = (res[...].astype(F32) + dot(po[...], mixed)).astype(BF16)

    for g in gw + gx + gst + [gpw, gow, gat]:
        g.drain()
    loop(1, npatch, lambda o: gln(o).drain())
    loop(1, npatch, lambda o: lncopy(o, band).wait_send())
    for layer in range(3):
        loop(1, npatch, lambda o: zcopy(layer, o).wait_send())
    for layer in range(2):
        @pl.when(has_below)
        def _():
            hcopy(layer, 0).wait_send()

        @pl.when(has_above)
        def _():
            hcopy(layer, 1).wait_send()


def local(
    npatch, nchan, nsub,
    latent, timestep, time_w1, time_proj, conv1_w, conv2_w, proj_in_w, q_w, kv_w, out_w, proj_out_w,
):
    own, tokens = latent.shape
    nheads = -(-own // HEAD_DIM)
    nidx = nchan * nsub
    temb = time_w1.shape[0]
    half_width = FREQ // 2
    frequency = jnp.exp(-math.log(10000.0) * jnp.arange(half_width, dtype=F32) / half_width)
    angles = timestep[0].astype(F32) * frequency
    embedded = jnp.concatenate([jnp.cos(angles), jnp.sin(angles)]).astype(BF16)
    emb = jnp.broadcast_to(embedded[None, :], (128, FREQ))
    vmem = pl.BlockSpec(memory_space=pltpu.VMEM)
    hbm = pl.BlockSpec(memory_space=pl.ANY)
    dma = pltpu.SemaphoreType.DMA
    span = nheads * HEAD_DIM
    ngather = G_LN + npatch
    return pl.pallas_call(
        functools.partial(kernel, npatch, nchan, nsub, own, nheads),
        out_shape=jax.ShapeDtypeStruct((own, tokens), BF16),
        in_specs=[vmem, vmem] + [hbm] * 9,
        out_specs=vmem,
        scratch_shapes=[
            pltpu.VMEM((temb, FREQ), BF16),
            pltpu.VMEM((own, temb), BF16),
            pltpu.VMEM((9, own, C), BF16),
            pltpu.VMEM((9, own, C), BF16),
            pltpu.VMEM((own, C), BF16),
        ]
        + [pltpu.VMEM((C, C), BF16)] * 5
        + [pltpu.VMEM((C, tokens), BF16)] * 4
        + [
            pltpu.VMEM((3, npatch, 8, 128), F32),
            pltpu.VMEM((3, nidx * 8, 128), F32),
            pltpu.VMEM((2, 2, own, tokens), BF16),
            pltpu.VMEM((2, 2, own, tokens), BF16),
            pltpu.VMEM((npatch, C, tokens), BF16),
            pltpu.VMEM((npatch, span, tokens), BF16),
            pltpu.VMEM((npatch, nheads, tokens, tokens), F32),
            pltpu.VMEM((span, tokens), BF16),
            pltpu.VMEM((C, tokens), BF16),
            pltpu.VMEM((own, tokens), BF16),
            dma((10,)),
            dma((ngather, nchan, nsub)),
            dma((ngather, nchan, nsub)),
            dma((3, npatch)),
            dma((3, npatch)),
            dma((2, 2)),
            dma((2, 2)),
            dma((npatch,)),
            dma((npatch,)),
        ],
        compiler_params=pltpu.CompilerParams(
            collective_id=0, has_side_effects=True, vmem_limit_bytes=60 * 1024 * 1024
        ),
    )(
        latent, emb, time_w1, time_proj, conv1_w, conv2_w, proj_in_w, q_w, kv_w, out_w, proj_out_w
    )


def solution(mesh):
    in_specs = (
        P(("chan", "sub"), ("groups", "patch")),
        P("groups"),
        P(),
        P(("chan", "sub"), None),
        P(None, ("chan", "sub"), None),
        P(None, ("chan", "sub"), None),
        P(("chan", "sub"), None),
        P(("chan", "sub"), None),
        P(None, ("chan", "sub"), None),
        P(("chan", "sub"), None),
        P(("chan", "sub"), None),
    )
    out_specs = P(("chan", "sub"), ("groups", "patch"))
    sizes = [mesh.shape[a] for a in ("patch", "chan", "sub")]
    return jax.shard_map(
        functools.partial(local, *sizes), mesh=mesh, in_specs=in_specs, out_specs=out_specs, check_vma=False
    )
```

```python
import functools
import math

import jax
import jax.numpy as jnp
from jax import lax
from jax.experimental import pallas as pl
from jax.experimental.pallas import tpu as pltpu
from jax.sharding import PartitionSpec as P

C = 640
HEADS = 10
HEAD_DIM = 64
NGROUPS = 32
FREQ = 320
WIDTH = 256
GROUP = C // NGROUPS
MESH = pl.DeviceIdType.MESH
F32 = jnp.float32
BF16 = jnp.bfloat16
HIGH = lax.Precision.HIGHEST

G_PW, G_OW, G_Q, G_K, G_V, G_X1, G_X2, G_X3, G_AT = range(9)
G_LN = 9


def dot(a, b, precision=None):
    return jnp.dot(a, b, preferred_element_type=F32, precision=precision)


def dot_nt(a, b):
    return lax.dot_general(a, b, (((1,), (1,)), ((), ())), preferred_element_type=F32)


def dot_tn(a, b):
    return lax.dot_general(a, b, (((0,), (0,)), ((), ())), preferred_element_type=F32)


def loop(low, high, body):
    if high - low <= 16:
        for k in range(low, high):
            body(k)
    else:
        lax.fori_loop(low, high, lambda k, _: (body(k), 0)[1], 0)


def silu(v):
    half = 0.5 * v
    return half + half * jnp.tanh(half)


def kernel(
    npatch, nchan, nsub, own, nheads,
    latent, emb, time_w1, time_proj, conv1_w, conv2_w, proj_in_w, q_w, kv_w, out_w, proj_out_w,
    out,
    tw1, tpj, cw1, cw2, po, pw, ow, qw, kw, vw, x1, x2, x3, at, zst, hsend, hrecv,
    ln, vals, scores, attn, proj, res,
    lsem, gsend, grecv, zsend, zrecv, hssem, hrsem, lnsend, lnrecv,
):
    band = lax.axis_index("patch")
    chan = lax.axis_index("chan")
    sub = lax.axis_index("sub")
    idx = chan * nsub + sub
    nidx = nchan * nsub
    tokens = latent.shape[1]
    aligned = (own * nsub) % HEAD_DIM == 0

    def rows(block, size):
        return pl.ds(pl.multiple_of(block * size, 16 if size % 16 == 0 else 8), size)

    mine = rows(idx, own)
    pairs = [
        (conv1_w, cw1), (time_w1, tw1), (time_proj, tpj), (q_w, qw.at[mine]),
        (kv_w.at[0], kw.at[mine]), (kv_w.at[1], vw.at[mine]), (proj_in_w, pw.at[mine]),
        (conv2_w, cw2), (out_w, ow.at[mine]), (proj_out_w, po),
    ]
    loads = [pltpu.make_async_copy(a, b, lsem.at[i]) for i, (a, b) in enumerate(pairs)]
    L_C1, L_T1, L_TP, L_Q, L_K, L_V, L_PW, L_C2, L_OW, L_PO = loads
    for load in loads:
        load.start()

    def other(k, by, count):
        return lax.rem(k + by + count, count)

    class Gather:
        def __init__(self, g, buf, size, only_sub=False):
            self.g, self.buf, self.size = g, buf, size
            self.chans = 1 if only_sub else nchan

        def copy(self, block, d, s):
            ref = self.buf.at[rows(block, self.size)]
            to = {"chan": other(chan, d, nchan)} if s == 0 else {"sub": other(sub, s, nsub)}
            return pltpu.make_async_remote_copy(
                src_ref=ref, dst_ref=ref, send_sem=gsend.at[self.g, d, s],
                recv_sem=grecv.at[self.g, d, s], device_id=to, device_id_type=MESH,
            )

        def start(self):
            for d in range(1, self.chans):
                self.copy(idx, d, 0).start()
            for s in range(1, nsub):
                self.copy(idx, 0, s).start()

        def forward(self):
            for d in range(1, self.chans):
                block = other(chan, -d, nchan) * nsub + sub
                self.copy(block, d, 0).wait_recv()
                for s in range(1, nsub):
                    self.copy(block, d, s).start()

        def finish(self):
            for d in range(self.chans):
                for s in range(1, nsub):
                    block = other(chan, -d, nchan) * nsub + other(sub, -s, nsub)
                    self.copy(block, d, s).wait_recv()

        def drain(self):
            for d in range(self.chans):
                for s in range(nsub):
                    if d or s:
                        self.copy(idx, d, s).wait_send()

    gw = [
        Gather(G_Q, qw, own, aligned), Gather(G_K, kw, own, aligned), Gather(G_V, vw, own, aligned),
    ]
    gpw, gow = Gather(G_PW, pw, own), Gather(G_OW, ow, own)
    gx = [Gather(G_X1, x1, own), Gather(G_X2, x2, own), Gather(G_X3, x3, own)]
    gat = Gather(G_AT, at, own)

    cell = GROUP * tokens

    def members(shape, group_dim, size):
        gi = lax.broadcasted_iota(jnp.int32, shape, group_dim)
        ci = lax.broadcasted_iota(jnp.int32, shape, 1 - group_dim)
        g = gi & 7
        first = (gi >> 3) * size + g * GROUP
        inside = (ci >= first) & (ci < first + GROUP) & (g < size // GROUP)
        return jnp.where(inside, 1.0, 0.0).astype(F32)

    def stats(x, layer):
        e = members((8, own), 0, own)
        et = members((own, 8), 1, own)
        mean = jnp.sum(dot(e, x, HIGH), axis=1, keepdims=True) * (1.0 / cell)
        mean = jnp.broadcast_to(mean, (8, 128))
        mc = dot(et, mean, HIGH)
        dev = x - jnp.concatenate([mc] * (tokens // 128), axis=1)
        m2 = jnp.sum(dot(e, dev * dev, HIGH), axis=1, keepdims=True)
        lane = lax.broadcasted_iota(jnp.int32, (8, 128), 1)
        zst[layer, band, rows(idx, 8)] = jnp.where(lane < 64, mean, m2)

    everyone = npatch * nidx

    def peer(p, way):
        k = p % nidx
        return {
            "patch": other(band, way * (p // nidx), npatch),
            "chan": other(chan, way * (k // nsub), nchan),
            "sub": other(sub, way * (k % nsub), nsub),
        }

    def zcopy(layer, p, source=None):
        b, k = (band, idx) if source is None else (source["patch"], source["chan"] * nsub + source["sub"])
        ref = zst.at[layer, b, rows(k, 8)]
        return pltpu.make_async_remote_copy(
            src_ref=ref, dst_ref=ref, send_sem=zsend.at[layer, p], recv_sem=zrecv.at[layer, p],
            device_id=peer(p, 1), device_id_type=MESH,
        )

    def share(layer):
        loop(1, everyone, lambda p: zcopy(layer, p).start())

    def combined(layer, eps):
        loop(1, everyone, lambda p: zcopy(layer, p, peer(p, -1)).wait_recv())
        tile = zst[layer]
        means, m2s = tile[:, :, 0:1], tile[:, :, 127:128]
        mean = jnp.sum(means, axis=0) * (1.0 / npatch)
        dev = means - mean[None]
        var = jnp.sum(m2s + cell * (dev * dev), axis=0) * (1.0 / (cell * npatch))
        shape = (nidx * 8, 128)
        lane = lax.broadcasted_iota(jnp.int32, shape, 1)
        pair = jnp.where(
            lane < 64, jnp.broadcast_to(mean, shape), jnp.broadcast_to(lax.rsqrt(var + eps), shape)
        )
        return dot(members((C, nidx * 8), 1, own), pair, HIGH)

    def normalize(x, both):
        return (x.astype(F32) - both[:, 0:1]) * both[:, 64:65]

    def hcopy(layer, way):
        return pltpu.make_async_remote_copy(
            src_ref=hsend.at[layer, way], dst_ref=hrecv.at[layer, way],
            send_sem=hssem.at[layer, way], recv_sem=hrsem.at[layer, way],
            device_id={"patch": other(band, 1 - 2 * way, npatch)}, device_id_type=MESH,
        )

    has_above, has_below = band > 0, band < npatch - 1

    def convolve(act, weight, layer):
        col = lax.broadcasted_iota(jnp.int32, act.shape, 1)
        taps = [
            jnp.where(col == 0, 0.0, pltpu.roll(act, 1, 1)).astype(BF16),
            act.astype(BF16),
            jnp.where(col == tokens - 1, 0.0, pltpu.roll(act, tokens - 1, 1)).astype(BF16),
        ]

        def row(i):
            return sum(dot(weight[3 * i + j], taps[j]) for j in range(3))

        hsend[layer, 0] = row(0).astype(BF16)

        @pl.when(has_below)
        def _():
            hcopy(layer, 0).start()

        hsend[layer, 1] = row(2).astype(BF16)

        @pl.when(has_above)
        def _():
            hcopy(layer, 1).start()

        return row(1)

    def neighbours(layer):
        @pl.when(has_above)
        def _():
            hcopy(layer, 0).wait_recv()

        @pl.when(has_below)
        def _():
            hcopy(layer, 1).wait_recv()

        return hrecv[layer, 0].astype(F32) + hrecv[layer, 1].astype(F32)

    for layer in range(2):
        @pl.when(jnp.logical_not(has_above))
        def _():
            hrecv[layer, 0] = jnp.zeros((own, tokens), BF16)

        @pl.when(jnp.logical_not(has_below))
        def _():
            hrecv[layer, 1] = jnp.zeros((own, tokens), BF16)

    barrier = pltpu.get_barrier_semaphore()
    loop(1, everyone, lambda p: pl.semaphore_signal(
        barrier, inc=1, device_id=peer(p, 1), device_id_type=MESH))
    x1[mine, :] = latent[...]
    lat = latent[...].astype(F32)
    stats(lat, 0)

    pl.semaphore_wait(barrier, everyone - 1)

    share(0)
    gx[0].start()
    L_T1.wait()
    hidden = silu(dot(emb[...], tw1[...]))
    L_TP.wait()
    bias = dot_nt(tpj[...], silu(hidden).astype(BF16))
    gx[0].forward()
    norm = combined(0, 1e-05)
    for load, g in zip((L_Q, L_K, L_V), gw):
        load.wait()
        g.start()
    gx[0].finish()
    L_PW.wait()
    gpw.start()
    L_C1.wait()
    centre = convolve(silu(normalize(x1[...], norm)), cw1, 0)
    conv_one = (centre + neighbours(0) + bias[:, 0:1]).astype(BF16)
    x2[mine, :] = conv_one
    stats(conv_one.astype(F32), 1)

    share(1)
    gx[1].start()
    gpw.forward()
    gx[1].forward()
    norm = combined(1, 1e-05)
    gx[1].finish()
    L_OW.wait()
    gow.start()
    L_C2.wait()
    centre = convolve(silu(normalize(x2[...], norm)), cw2, 1)
    resnet = (lat + (centre + neighbours(1))).astype(BF16)
    res[...] = resnet
    x3[mine, :] = resnet
    stats(resnet.astype(F32), 2)

    share(2)
    gx[2].start()
    gow.forward()
    gx[2].forward()
    norm = combined(2, 1e-06)
    gpw.finish()
    gx[2].finish()
    projected = dot(pw[...], normalize(x3[...], norm).astype(BF16)).astype(BF16)
    proj[...] = projected
    wide = projected.astype(F32)
    wide = wide - jnp.mean(wide, axis=0, keepdims=True)
    spread = jnp.mean(wide * wide, axis=0, keepdims=True)
    ln[band] = (wide * lax.rsqrt(spread + 1e-05)).astype(BF16)

    def lncopy(o, source):
        ref = ln.at[source, mine]
        return pltpu.make_async_remote_copy(
            src_ref=ref, dst_ref=ref, send_sem=lnsend.at[o], recv_sem=lnrecv.at[o],
            device_id={"patch": other(band, o, npatch)}, device_id_type=MESH,
        )

    def gln(o):
        return Gather(G_LN + o, ln.at[other(band, -o, npatch)], own)

    loop(1, npatch, lambda o: lncopy(o, band).start())
    for g in gw:
        if not aligned:
            g.forward()
        g.finish()

    head0 = (idx * own) // HEAD_DIM
    span = nheads * HEAD_DIM
    held = pl.ds(pl.multiple_of(head0 * HEAD_DIM, HEAD_DIM), span)
    query = (dot(qw[held, :], ln[band]) * 0.125).astype(BF16)

    def score(source):
        tokens_of = ln[source]
        keys = dot(kw[held, :], tokens_of).astype(BF16)
        vals[source] = dot(vw[held, :], tokens_of).astype(BF16)
        for h in range(nheads):
            part = slice(h * HEAD_DIM, (h + 1) * HEAD_DIM)
            scores[source, h] = dot_tn(keys[part], query[part])

    def relay(o):
        lncopy(o, other(band, -o, npatch)).wait_recv()
        gln(o).start()

    score(band)
    loop(1, npatch, relay)
    loop(1, npatch, lambda o: gln(o).forward())

    def arrive(o):
        gln(o).finish()
        score(other(band, -o, npatch))

    loop(1, npatch, arrive)

    for h in range(nheads):
        part = slice(h * HEAD_DIM, (h + 1) * HEAD_DIM)

        def peak_of(b, peak):
            return jnp.maximum(peak, jnp.max(scores[b, h], axis=0, keepdims=True))

        def add(b, so_far):
            total, weighted = so_far
            weights = jnp.exp(scores[b, h] - peak)
            total = total + jnp.sum(weights, axis=0, keepdims=True)
            return total, weighted + dot(vals[b, part], weights.astype(BF16))

        peak = jnp.full((1, tokens), -jnp.inf, F32)
        so_far = (jnp.zeros((1, tokens), F32), jnp.zeros((HEAD_DIM, tokens), F32))
        if npatch <= 4:
            for b in range(npatch):
                peak = peak_of(b, peak)
            for b in range(npatch):
                so_far = add(b, so_far)
        else:
            peak = lax.fori_loop(0, npatch, peak_of, peak)
            so_far = lax.fori_loop(0, npatch, add, so_far)
        attn[part, :] = (so_far[1] / so_far[0]).astype(BF16)

    skip = pl.multiple_of(idx * own - head0 * HEAD_DIM, 16)
    at[mine, :] = attn[pl.ds(skip, own), :]
    gat.start()
    gat.forward()
    gow.finish()
    gat.finish()
    mixed = (proj[...].astype(F32) + dot(ow[...], at[...])).astype(BF16)
    L_PO.wait()
    out[...] = res[...].astype(F32) + dot(po[...], mixed)

    for g in gw + gx + [gpw, gow, gat]:
        g.drain()
    loop(1, npatch, lambda o: gln(o).drain())
    loop(1, npatch, lambda o: lncopy(o, band).wait_send())
    for layer in range(3):
        loop(1, everyone, lambda p: zcopy(layer, p).wait_send())
    for layer in range(2):
        @pl.when(has_below)
        def _():
            hcopy(layer, 0).wait_send()

        @pl.when(has_above)
        def _():
            hcopy(layer, 1).wait_send()


def local(
    npatch, nchan, nsub,
    latent, timestep, time_w1, time_proj, conv1_w, conv2_w, proj_in_w, q_w, kv_w, out_w, proj_out_w,
):
    own, tokens = latent.shape
    nheads = -(-own // HEAD_DIM)
    nidx = nchan * nsub
    temb = time_w1.shape[0]
    half_width = FREQ // 2
    frequency = jnp.exp(-math.log(10000.0) * jnp.arange(half_width, dtype=F32) / half_width)
    angles = timestep[0].astype(F32) * frequency
    embedded = jnp.concatenate([jnp.cos(angles), jnp.sin(angles)]).astype(BF16)
    emb = jnp.broadcast_to(embedded[None, :], (16, FREQ))
    vmem = pl.BlockSpec(memory_space=pltpu.VMEM)
    hbm = pl.BlockSpec(memory_space=pl.ANY)
    dma = pltpu.SemaphoreType.DMA
    span = nheads * HEAD_DIM
    ngather = G_LN + npatch
    total = pl.pallas_call(
        functools.partial(kernel, npatch, nchan, nsub, own, nheads),
        out_shape=jax.ShapeDtypeStruct((own, tokens), F32),
        in_specs=[vmem, vmem] + [hbm] * 9,
        out_specs=vmem,
        scratch_shapes=[
            pltpu.VMEM((FREQ, temb), BF16),
            pltpu.VMEM((own, temb), BF16),
            pltpu.VMEM((9, own, C), BF16),
            pltpu.VMEM((9, own, C), BF16),
            pltpu.VMEM((own, C), BF16),
        ]
        + [pltpu.VMEM((C, C), BF16)] * 5
        + [pltpu.VMEM((C, tokens), BF16)] * 4
        + [
            pltpu.VMEM((3, npatch, nidx * 8, 128), F32),
            pltpu.VMEM((2, 2, own, tokens), BF16),
            pltpu.VMEM((2, 2, own, tokens), BF16),
            pltpu.VMEM((npatch, C, tokens), BF16),
            pltpu.VMEM((npatch, span, tokens), BF16),
            pltpu.VMEM((npatch, nheads, tokens, tokens), F32),
            pltpu.VMEM((span, tokens), BF16),
            pltpu.VMEM((C, tokens), BF16),
            pltpu.VMEM((own, tokens), BF16),
            dma((10,)),
            dma((ngather, nchan, nsub)),
            dma((ngather, nchan, nsub)),
            dma((3, npatch * nidx)),
            dma((3, npatch * nidx)),
            dma((2, 2)),
            dma((2, 2)),
            dma((npatch,)),
            dma((npatch,)),
        ],
        compiler_params=pltpu.CompilerParams(
            collective_id=0, has_side_effects=True, vmem_limit_bytes=60 * 1024 * 1024
        ),
    )(
        latent, emb, time_w1.T, time_proj, conv1_w, conv2_w, proj_in_w, q_w, kv_w, out_w, proj_out_w
    )
    return total.astype(BF16)


def solution(mesh):
    in_specs = (
        P(("chan", "sub"), ("groups", "patch")),
        P("groups"),
        P(),
        P(("chan", "sub"), None),
        P(None, ("chan", "sub"), None),
        P(None, ("chan", "sub"), None),
        P(("chan", "sub"), None),
        P(("chan", "sub"), None),
        P(None, ("chan", "sub"), None),
        P(("chan", "sub"), None),
        P(("chan", "sub"), None),
    )
    out_specs = P(("chan", "sub"), ("groups", "patch"))
    sizes = [mesh.shape[a] for a in ("patch", "chan", "sub")]
    return jax.shard_map(
        functools.partial(local, *sizes), mesh=mesh, in_specs=in_specs, out_specs=out_specs, check_vma=False
    )
```

```python
import functools
import math

import jax
import jax.numpy as jnp
from jax import lax
from jax.experimental import pallas as pl
from jax.experimental.pallas import tpu as pltpu
from jax.sharding import PartitionSpec as P

C = 640
HEADS = 10
HEAD_DIM = 64
NGROUPS = 32
FREQ = 320
WIDTH = 256
GROUP = C // NGROUPS
MESH = pl.DeviceIdType.MESH
F32 = jnp.float32
BF16 = jnp.bfloat16
HIGH = lax.Precision.HIGHEST

G_PW, G_OW, G_Q, G_K, G_V, G_X1, G_X2, G_AT = range(8)
G_LN = 8


def dot(a, b, precision=None):
    return jnp.dot(a, b, preferred_element_type=F32, precision=precision)


def dot_nt(a, b):
    return lax.dot_general(a, b, (((1,), (1,)), ((), ())), preferred_element_type=F32)


def dot_tn(a, b):
    return lax.dot_general(a, b, (((0,), (0,)), ((), ())), preferred_element_type=F32)


def loop(low, high, body):
    if high - low <= 16:
        for k in range(low, high):
            body(k)
    else:
        lax.fori_loop(low, high, lambda k, _: (body(k), 0)[1], 0)


def silu(v):
    half = 0.5 * v
    return half + half * jnp.tanh(half)


def kernel(
    npatch, nchan, nsub, own, nheads,
    latent, emb, time_w1, time_proj, conv1_w, conv2_w, proj_in_w, q_w, kv_w, out_w, proj_out_w,
    out,
    tw1, tpj, cw1, cw2, po, pw, ow, qw, kw, vw, x1, x2, at, zst, hsend, hrecv,
    xr, qry, peaks, totals, sums, attn, proj, res,
    lsem, gsend, grecv, zsend, zrecv, hssem, hrsem, lnsend, lnrecv,
):
    band = lax.axis_index("patch")
    chan = lax.axis_index("chan")
    sub = lax.axis_index("sub")
    idx = chan * nsub + sub
    nidx = nchan * nsub
    tokens = latent.shape[1]
    aligned = (own * nsub) % HEAD_DIM == 0

    def rows(block, size):
        return pl.ds(pl.multiple_of(block * size, 16 if size % 16 == 0 else 8), size)

    mine = rows(idx, own)
    pairs = [
        (conv1_w, cw1), (time_w1, tw1), (time_proj, tpj), (q_w, qw.at[mine]),
        (kv_w.at[0], kw.at[mine]), (kv_w.at[1], vw.at[mine]), (proj_in_w, pw.at[mine]),
        (conv2_w, cw2), (out_w, ow.at[mine]), (proj_out_w, po),
    ]
    loads = [pltpu.make_async_copy(a, b, lsem.at[i]) for i, (a, b) in enumerate(pairs)]
    L_C1, L_T1, L_TP, L_Q, L_K, L_V, L_PW, L_C2, L_OW, L_PO = loads
    for load in loads:
        load.start()

    def other(k, by, count):
        return lax.rem(k + by + count, count)

    class Gather:
        def __init__(self, g, buf, size, only_sub=False):
            self.g, self.buf, self.size = g, buf, size
            self.chans = 1 if only_sub else nchan

        def copy(self, block, d, s):
            ref = self.buf.at[rows(block, self.size)]
            to = {"chan": other(chan, d, nchan)} if s == 0 else {"sub": other(sub, s, nsub)}
            return pltpu.make_async_remote_copy(
                src_ref=ref, dst_ref=ref, send_sem=gsend.at[self.g, d, s],
                recv_sem=grecv.at[self.g, d, s], device_id=to, device_id_type=MESH,
            )

        def start(self):
            for d in range(1, self.chans):
                self.copy(idx, d, 0).start()
            for s in range(1, nsub):
                self.copy(idx, 0, s).start()

        def forward(self):
            for d in range(1, self.chans):
                block = other(chan, -d, nchan) * nsub + sub
                self.copy(block, d, 0).wait_recv()
                for s in range(1, nsub):
                    self.copy(block, d, s).start()

        def finish(self):
            for d in range(self.chans):
                for s in range(1, nsub):
                    block = other(chan, -d, nchan) * nsub + other(sub, -s, nsub)
                    self.copy(block, d, s).wait_recv()

        def drain(self):
            for d in range(self.chans):
                for s in range(nsub):
                    if d or s:
                        self.copy(idx, d, s).wait_send()

    gw = [
        Gather(G_Q, qw, own, aligned), Gather(G_K, kw, own, aligned), Gather(G_V, vw, own, aligned),
    ]
    gpw, gow = Gather(G_PW, pw, own), Gather(G_OW, ow, own)
    gx = [Gather(G_X1, x1, own), Gather(G_X2, x2, own)]
    gat = Gather(G_AT, at, own)

    cell = GROUP * tokens

    def members(shape, group_dim, size):
        gi = lax.broadcasted_iota(jnp.int32, shape, group_dim)
        ci = lax.broadcasted_iota(jnp.int32, shape, 1 - group_dim)
        g = gi & 7
        first = (gi >> 3) * size + g * GROUP
        inside = (ci >= first) & (ci < first + GROUP) & (g < size // GROUP)
        return jnp.where(inside, 1.0, 0.0).astype(F32)

    def stats(x, layer):
        e = members((8, own), 0, own)
        et = members((own, 8), 1, own)
        mean = jnp.sum(dot(e, x, HIGH), axis=1, keepdims=True) * (1.0 / cell)
        mean = jnp.broadcast_to(mean, (8, 128))
        mc = dot(et, mean, HIGH)
        dev = x - jnp.concatenate([mc] * (tokens // 128), axis=1)
        m2 = jnp.sum(dot(e, dev * dev, HIGH), axis=1, keepdims=True)
        lane = lax.broadcasted_iota(jnp.int32, (8, 128), 1)
        zst[layer, band, rows(idx, 8)] = jnp.where(lane < 64, mean, m2)

    everyone = npatch * nidx

    def peer(p, way):
        k = p % nidx
        return {
            "patch": other(band, way * (p // nidx), npatch),
            "chan": other(chan, way * (k // nsub), nchan),
            "sub": other(sub, way * (k % nsub), nsub),
        }

    def zcopy(layer, p, source=None):
        b, k = (band, idx) if source is None else (source["patch"], source["chan"] * nsub + source["sub"])
        ref = zst.at[layer, b, rows(k, 8)]
        return pltpu.make_async_remote_copy(
            src_ref=ref, dst_ref=ref, send_sem=zsend.at[layer, p], recv_sem=zrecv.at[layer, p],
            device_id=peer(p, 1), device_id_type=MESH,
        )

    def share(layer):
        loop(1, everyone, lambda p: zcopy(layer, p).start())

    def combined(layer, eps):
        loop(1, everyone, lambda p: zcopy(layer, p, peer(p, -1)).wait_recv())
        tile = zst[layer]
        means, m2s = tile[:, :, 0:1], tile[:, :, 127:128]
        mean = jnp.sum(means, axis=0) * (1.0 / npatch)
        dev = means - mean[None]
        var = jnp.sum(m2s + cell * (dev * dev), axis=0) * (1.0 / (cell * npatch))
        shape = (nidx * 8, 128)
        lane = lax.broadcasted_iota(jnp.int32, shape, 1)
        pair = jnp.where(
            lane < 64, jnp.broadcast_to(mean, shape), jnp.broadcast_to(lax.rsqrt(var + eps), shape)
        )
        return dot(members((C, nidx * 8), 1, own), pair, HIGH)

    def normalize(x, both):
        return (x.astype(F32) - both[:, 0:1]) * both[:, 64:65]

    def hcopy(layer, way):
        return pltpu.make_async_remote_copy(
            src_ref=hsend.at[layer, way], dst_ref=hrecv.at[layer, way],
            send_sem=hssem.at[layer, way], recv_sem=hrsem.at[layer, way],
            device_id={"patch": other(band, 1 - 2 * way, npatch)}, device_id_type=MESH,
        )

    has_above, has_below = band > 0, band < npatch - 1

    def convolve(act, weight, layer):
        col = lax.broadcasted_iota(jnp.int32, act.shape, 1)
        taps = [
            jnp.where(col == 0, 0.0, pltpu.roll(act, 1, 1)).astype(BF16),
            act.astype(BF16),
            jnp.where(col == tokens - 1, 0.0, pltpu.roll(act, tokens - 1, 1)).astype(BF16),
        ]

        def row(i):
            return sum(dot(weight[3 * i + j], taps[j]) for j in range(3))

        hsend[layer, 0] = row(0).astype(BF16)

        @pl.when(has_below)
        def _():
            hcopy(layer, 0).start()

        hsend[layer, 1] = row(2).astype(BF16)

        @pl.when(has_above)
        def _():
            hcopy(layer, 1).start()

        return row(1)

    def neighbours(layer):
        @pl.when(has_above)
        def _():
            hcopy(layer, 0).wait_recv()

        @pl.when(has_below)
        def _():
            hcopy(layer, 1).wait_recv()

        return hrecv[layer, 0].astype(F32) + hrecv[layer, 1].astype(F32)

    for layer in range(2):
        @pl.when(jnp.logical_not(has_above))
        def _():
            hrecv[layer, 0] = jnp.zeros((own, tokens), BF16)

        @pl.when(jnp.logical_not(has_below))
        def _():
            hrecv[layer, 1] = jnp.zeros((own, tokens), BF16)

    barrier = pltpu.get_barrier_semaphore()
    loop(1, everyone, lambda p: pl.semaphore_signal(
        barrier, inc=1, device_id=peer(p, 1), device_id_type=MESH))
    x1[mine, :] = latent[...]
    lat = latent[...].astype(F32)
    stats(lat, 0)

    pl.semaphore_wait(barrier, everyone - 1)

    share(0)
    gx[0].start()
    L_T1.wait()
    hidden = silu(dot(emb[...], tw1[...]))
    L_TP.wait()
    bias = dot_nt(tpj[...], silu(hidden).astype(BF16))
    gx[0].forward()
    norm = combined(0, 1e-05)
    for load, g in zip((L_Q, L_K, L_V), gw):
        load.wait()
        g.start()
    gx[0].finish()
    L_PW.wait()
    gpw.start()
    L_C1.wait()
    centre = convolve(silu(normalize(x1[...], norm)), cw1, 0)
    conv_one = (centre + neighbours(0) + bias[:, 0:1]).astype(BF16)
    x2[mine, :] = conv_one
    stats(conv_one.astype(F32), 1)

    share(1)
    gx[1].start()
    gpw.forward()
    gx[1].forward()
    norm = combined(1, 1e-05)
    gx[1].finish()
    L_OW.wait()
    gow.start()
    L_C2.wait()
    centre = convolve(silu(normalize(x2[...], norm)), cw2, 1)
    resnet = (lat + (centre + neighbours(1))).astype(BF16)
    res[...] = resnet
    xr[band, mine, :] = resnet

    def zrow(to, source):
        ref = xr.at[source, mine]
        return pltpu.make_async_remote_copy(
            src_ref=ref, dst_ref=ref, send_sem=lnsend.at[to], recv_sem=lnrecv.at[source],
            device_id={"patch": to}, device_id_type=MESH,
        )

    def grow(source):
        return Gather(G_LN + source, xr.at[source], own)

    def nearest(rank):
        near = jnp.minimum(band, npatch - 1 - band)
        odd = rank % 2
        step = (rank + odd) // 2
        beyond = jnp.where(2 * band < npatch - 1, rank, npatch - 1 - rank)
        return jnp.where(rank <= 2 * near, band + (1 - 2 * odd) * step, beyond)

    grow(band).start()
    loop(1, npatch, lambda r: zrow(nearest(r), band).start())
    stats(resnet.astype(F32), 2)
    share(2)
    grow(band).forward()
    gow.forward()
    gpw.finish()
    for g in gw:
        if not aligned:
            g.forward()
        g.finish()
    norm = combined(2, 1e-06)
    grow(band).finish()

    head0 = (idx * own) // HEAD_DIM
    span = nheads * HEAD_DIM
    held = pl.ds(pl.multiple_of(head0 * HEAD_DIM, HEAD_DIM), span)

    def project(source):
        projected = dot(pw[...], normalize(xr[source], norm).astype(BF16)).astype(BF16)
        wide = projected.astype(F32)
        wide = wide - jnp.mean(wide, axis=0, keepdims=True)
        spread = jnp.mean(wide * wide, axis=0, keepdims=True)
        return projected, (wide * lax.rsqrt(spread + 1e-05)).astype(BF16)

    def attend(normed, query, first):
        keys = dot(kw[held, :], normed).astype(BF16)
        values = dot(vw[held, :], normed).astype(BF16)
        for h in range(nheads):
            part = slice(h * HEAD_DIM, (h + 1) * HEAD_DIM)
            scores = dot_tn(keys[part], query[part])
            peak = jnp.max(scores, axis=0, keepdims=True)
            if not first:
                old = peaks[h]
                peak = jnp.maximum(peak, old)
                factor = jnp.exp(old - peak)
            weights = jnp.exp(scores - peak)
            total = jnp.sum(weights, axis=0, keepdims=True)
            update = dot(values[part], weights.astype(BF16))
            if not first:
                total = total + totals[h] * factor
                update = update + sums[part, :] * factor
            peaks[h] = peak
            totals[h] = total
            sums[part, :] = update

    def relay(rank):
        source = nearest(rank)
        zrow(source, source).wait_recv()
        grow(source).start()

    relay(1)
    projected, normed = project(band)
    proj[...] = projected
    qry[...] = (dot(qw[held, :], normed) * 0.125).astype(BF16)
    if npatch > 2:
        relay(2)
    grow(nearest(1)).forward()
    attend(normed, qry[...], True)

    def arrive(rank):
        source = nearest(rank)
        grow(source).finish()
        attend(project(source)[1], qry[...], False)

    for rank in range(1, min(npatch, 3)):
        if rank + 2 < npatch:
            relay(rank + 2)
        if rank + 1 < npatch:
            grow(nearest(rank + 1)).forward()
        arrive(rank)

    def further(rank):
        if npatch > 4:
            @pl.when(rank + 2 < npatch)
            def _():
                relay(rank + 2)

            @pl.when(rank + 1 < npatch)
            def _():
                grow(nearest(rank + 1)).forward()
        arrive(rank)

    loop(3, npatch, further)
    for h in range(nheads):
        part = slice(h * HEAD_DIM, (h + 1) * HEAD_DIM)
        attn[part, :] = (sums[part, :] / totals[h]).astype(BF16)

    skip = pl.multiple_of(idx * own - head0 * HEAD_DIM, 16)
    at[mine, :] = attn[pl.ds(skip, own), :]
    gat.start()
    gat.forward()
    gow.finish()
    gat.finish()
    mixed = (proj[...].astype(F32) + dot(ow[...], at[...])).astype(BF16)
    L_PO.wait()
    out[...] = res[...].astype(F32) + dot(po[...], mixed)

    for g in gw + gx + [gpw, gow, gat]:
        g.drain()
    loop(0, npatch, lambda b: grow(b).drain())
    loop(1, npatch, lambda r: zrow(nearest(r), band).wait_send())
    for layer in range(3):
        loop(1, everyone, lambda p: zcopy(layer, p).wait_send())
    for layer in range(2):
        @pl.when(has_below)
        def _():
            hcopy(layer, 0).wait_send()

        @pl.when(has_above)
        def _():
            hcopy(layer, 1).wait_send()


def local(
    npatch, nchan, nsub,
    latent, timestep, time_w1, time_proj, conv1_w, conv2_w, proj_in_w, q_w, kv_w, out_w, proj_out_w,
):
    own, tokens = latent.shape
    nheads = -(-own // HEAD_DIM)
    nidx = nchan * nsub
    temb = time_w1.shape[0]
    half_width = FREQ // 2
    frequency = jnp.exp(-math.log(10000.0) * jnp.arange(half_width, dtype=F32) / half_width)
    angles = timestep[0].astype(F32) * frequency
    embedded = jnp.concatenate([jnp.cos(angles), jnp.sin(angles)]).astype(BF16)
    emb = jnp.broadcast_to(embedded[None, :], (16, FREQ))
    vmem = pl.BlockSpec(memory_space=pltpu.VMEM)
    hbm = pl.BlockSpec(memory_space=pl.ANY)
    dma = pltpu.SemaphoreType.DMA
    span = nheads * HEAD_DIM
    ngather = G_LN + npatch
    total = pl.pallas_call(
        functools.partial(kernel, npatch, nchan, nsub, own, nheads),
        out_shape=jax.ShapeDtypeStruct((own, tokens), F32),
        in_specs=[vmem, vmem] + [hbm] * 9,
        out_specs=vmem,
        scratch_shapes=[
            pltpu.VMEM((FREQ, temb), BF16),
            pltpu.VMEM((own, temb), BF16),
            pltpu.VMEM((9, own, C), BF16),
            pltpu.VMEM((9, own, C), BF16),
            pltpu.VMEM((own, C), BF16),
        ]
        + [pltpu.VMEM((C, C), BF16)] * 5
        + [pltpu.VMEM((C, tokens), BF16)] * 3
        + [
            pltpu.VMEM((3, npatch, nidx * 8, 128), F32),
            pltpu.VMEM((2, 2, own, tokens), BF16),
            pltpu.VMEM((2, 2, own, tokens), BF16),
            pltpu.VMEM((npatch, C, tokens), BF16),
            pltpu.VMEM((span, tokens), BF16),
            pltpu.VMEM((nheads, 1, tokens), F32),
            pltpu.VMEM((nheads, 1, tokens), F32),
            pltpu.VMEM((span, tokens), F32),
            pltpu.VMEM((span, tokens), BF16),
            pltpu.VMEM((C, tokens), BF16),
            pltpu.VMEM((own, tokens), BF16),
            dma((10,)),
            dma((ngather, nchan, nsub)),
            dma((ngather, nchan, nsub)),
            dma((3, npatch * nidx)),
            dma((3, npatch * nidx)),
            dma((2, 2)),
            dma((2, 2)),
            dma((npatch,)),
            dma((npatch,)),
        ],
        compiler_params=pltpu.CompilerParams(
            collective_id=0, has_side_effects=True, vmem_limit_bytes=60 * 1024 * 1024
        ),
    )(
        latent, emb, time_w1.T, time_proj, conv1_w, conv2_w, proj_in_w, q_w, kv_w, out_w, proj_out_w
    )
    return total.astype(BF16)


def solution(mesh):
    in_specs = (
        P(("chan", "sub"), ("groups", "patch")),
        P("groups"),
        P(),
        P(("chan", "sub"), None),
        P(None, ("chan", "sub"), None),
        P(None, ("chan", "sub"), None),
        P(("chan", "sub"), None),
        P(("chan", "sub"), None),
        P(None, ("chan", "sub"), None),
        P(("chan", "sub"), None),
        P(("chan", "sub"), None),
    )
    out_specs = P(("chan", "sub"), ("groups", "patch"))
    sizes = [mesh.shape[a] for a in ("patch", "chan", "sub")]
    return jax.shard_map(
        functools.partial(local, *sizes), mesh=mesh, in_specs=in_specs, out_specs=out_specs, check_vma=False
    )
```

```python
import functools
import math

import jax
import jax.numpy as jnp
from jax import lax
from jax.experimental import pallas as pl
from jax.experimental.pallas import tpu as pltpu
from jax.sharding import PartitionSpec as P

C = 640
HEADS = 10
HEAD_DIM = 64
NGROUPS = 32
FREQ = 320
WIDTH = 256
GROUP = C // NGROUPS
MESH = pl.DeviceIdType.MESH
F32 = jnp.float32
BF16 = jnp.bfloat16
HIGH = lax.Precision.HIGHEST

G_PW, G_OW, G_Q, G_K, G_V, G_X1, G_X2, G_X3, G_AT = range(9)
G_LN = 9


def dot(a, b, precision=None):
    return jnp.dot(a, b, preferred_element_type=F32, precision=precision)


def dot_nt(a, b):
    return lax.dot_general(a, b, (((1,), (1,)), ((), ())), preferred_element_type=F32)


def dot_tn(a, b):
    return lax.dot_general(a, b, (((0,), (0,)), ((), ())), preferred_element_type=F32)


def loop(low, high, body):
    if high - low <= 16:
        for k in range(low, high):
            body(k)
    else:
        lax.fori_loop(low, high, lambda k, _: (body(k), 0)[1], 0)


def silu(v):
    half = 0.5 * v
    return half + half * jnp.tanh(half)


def kernel(
    npatch, nchan, nsub, own, nheads,
    latent, emb, time_w1, time_proj, conv1_w, conv2_w, proj_in_w, q_w, kv_w, out_w, proj_out_w,
    out,
    tw1, tpj, cw1, cw2, po, pw, ow, qw, kw, vw, x1, x2, x3, at, e16, et16, spread_w, zst, hsend, hrecv,
    xr, qry, peaks, totals, sums, attn, proj, res,
    lsem, gsend, grecv, zsend, zrecv, hssem, hrsem, lnsend, lnrecv,
):
    band = lax.axis_index("patch")
    chan = lax.axis_index("chan")
    sub = lax.axis_index("sub")
    idx = chan * nsub + sub
    nidx = nchan * nsub
    tokens = latent.shape[1]
    aligned = (own * nsub) % HEAD_DIM == 0

    def rows(block, size):
        return pl.ds(pl.multiple_of(block * size, 16 if size % 16 == 0 else 8), size)

    mine = rows(idx, own)
    pairs = [
        (time_w1, tw1), (time_proj, tpj), (q_w, qw.at[mine]), (kv_w.at[0], kw.at[mine]),
        (kv_w.at[1], vw.at[mine]), (proj_in_w, pw.at[mine]), (out_w, ow.at[mine]), (proj_out_w, po),
    ]
    for held, weight in ((conv1_w, cw1), (conv2_w, cw2)):
        for tap in range(9):
            place = (0, 2, 1)[tap // 3]
            part = weight.at[pl.ds(place * own, own), pl.ds(tap % 3 * C, C)]
            pairs.append((held.at[tap], part))
    loads = [pltpu.make_async_copy(a, b, lsem.at[i]) for i, (a, b) in enumerate(pairs)]
    L_T1, L_TP, L_Q, L_K, L_V, L_PW, L_OW, L_PO = loads[:8]
    L_CONV = (loads[8:17], loads[17:26])
    for load in loads[:2] + L_CONV[0] + loads[2:8] + L_CONV[1]:
        load.start()

    def other(k, by, count):
        to = k + by + count
        to = jnp.where(to >= 2 * count, to - 2 * count, to)
        return jnp.where(to >= count, to - count, to)

    class Gather:
        def __init__(self, g, buf, size, only_sub=False):
            self.g, self.buf, self.size = g, buf, size
            self.chans = 1 if only_sub else nchan

        def copy(self, block, d, s):
            ref = self.buf.at[rows(block, self.size)]
            to = {"chan": other(chan, d, nchan)} if s == 0 else {"sub": other(sub, s, nsub)}
            return pltpu.make_async_remote_copy(
                src_ref=ref, dst_ref=ref, send_sem=gsend.at[self.g, d, s],
                recv_sem=grecv.at[self.g, d, s], device_id=to, device_id_type=MESH,
            )

        def start(self):
            for d in range(1, self.chans):
                self.copy(idx, d, 0).start()
            for s in range(1, nsub):
                self.copy(idx, 0, s).start()

        def forward(self):
            for d in range(1, self.chans):
                block = other(chan, -d, nchan) * nsub + sub
                self.copy(block, d, 0).wait_recv()
                for s in range(1, nsub):
                    self.copy(block, d, s).start()

        def finish(self):
            for d in range(self.chans):
                for s in range(1, nsub):
                    block = other(chan, -d, nchan) * nsub + other(sub, -s, nsub)
                    self.copy(block, d, s).wait_recv()

        def drain(self):
            for d in range(self.chans):
                for s in range(nsub):
                    if d or s:
                        self.copy(idx, d, s).wait_send()

    gw = [
        Gather(G_Q, qw, own, aligned), Gather(G_K, kw, own, aligned), Gather(G_V, vw, own, aligned),
    ]
    gpw, gow = Gather(G_PW, pw, own), Gather(G_OW, ow, own)
    gx = [Gather(G_X1, x1, own), Gather(G_X2, x2, own), Gather(G_X3, x3, own)]
    gat = Gather(G_AT, at, own)

    cell = GROUP * tokens

    def members(shape, group_dim, size, times=1):
        gi = lax.broadcasted_iota(jnp.int32, shape, group_dim)
        ci = lax.broadcasted_iota(jnp.int32, shape, 1 - group_dim)
        period = shape[group_dim] // times
        for k in range(times - 1, 0, -1):
            gi = jnp.where(gi >= k * period, gi - k * period, gi)
        g = gi & 7
        first = (gi >> 3) * size + g * GROUP
        inside = (ci >= first) & (ci < first + GROUP) & (g < size // GROUP)
        return jnp.where(inside, 1.0, 0.0).astype(BF16)

    def stats(x, layer):
        mean = jnp.sum(dot(e16[...], x), axis=1, keepdims=True) * (1.0 / cell)
        mean = jnp.broadcast_to(mean, (16, 128))
        shift = mean.astype(BF16)
        sc = dot(et16[...], shift)
        sq = jnp.zeros((own, 128), F32)
        for k in range(0, tokens, 128):
            dev = x[:, k : k + 128].astype(F32) - sc
            sq = sq + dev * dev
        hi = sq.astype(BF16)
        lo = (sq - hi.astype(F32)).astype(BF16)
        m2 = jnp.sum(dot(e16[...], jnp.concatenate([hi, lo], axis=1)), axis=1, keepdims=True)
        gap = mean - shift.astype(F32)
        m2 = jnp.maximum(m2 - cell * (gap * gap), 0.0)
        lane = lax.broadcasted_iota(jnp.int32, (16, 128), 1)
        zst[layer, band, rows(idx, 8)] = jnp.where(lane < 64, mean, m2)[0:8]

    everyone = npatch * nidx

    def peer(p, way):
        k = p % nidx
        return {
            "patch": other(band, way * (p // nidx), npatch),
            "chan": other(chan, way * (k // nsub), nchan),
            "sub": other(sub, way * (k % nsub), nsub),
        }

    def zcopy(layer, p, source=None):
        b, k = (band, idx) if source is None else (source["patch"], source["chan"] * nsub + source["sub"])
        ref = zst.at[layer, b, rows(k, 8)]
        return pltpu.make_async_remote_copy(
            src_ref=ref, dst_ref=ref, send_sem=zsend.at[layer, p], recv_sem=zrecv.at[layer, p],
            device_id=peer(p, 1), device_id_type=MESH,
        )

    def share(layer):
        loop(1, everyone, lambda p: zcopy(layer, p).start())

    def combined(layer, eps):
        loop(1, everyone, lambda p: zcopy(layer, p, peer(p, -1)).wait_recv())
        tile = zst[layer]
        means, m2s = tile[:, :, 0:1], tile[:, :, 127:128]
        mean = jnp.sum(means, axis=0) * (1.0 / npatch)
        dev = means - mean[None]
        var = jnp.sum(m2s + cell * (dev * dev), axis=0) * (1.0 / (cell * npatch))
        shape = (nidx * 8, 128)
        lane = lax.broadcasted_iota(jnp.int32, shape, 1)
        pair = jnp.where(
            lane < 64, jnp.broadcast_to(mean, shape), jnp.broadcast_to(lax.rsqrt(var + eps), shape)
        )
        one = pair.astype(BF16)
        rest = pair - one.astype(F32)
        two = rest.astype(BF16)
        three = (rest - two.astype(F32)).astype(BF16)
        return dot(spread_w[...], jnp.concatenate([one, two, three], axis=0))

    def normalize(x, both):
        return (x.astype(F32) - both[:, 0:1]) * both[:, 64:65]

    def hcopy(layer, way):
        return pltpu.make_async_remote_copy(
            src_ref=hsend.at[layer, way], dst_ref=hrecv.at[layer, way],
            send_sem=hssem.at[layer, way], recv_sem=hrsem.at[layer, way],
            device_id={"patch": other(band, 1 - 2 * way, npatch)}, device_id_type=MESH,
        )

    has_above, has_below = band > 0, band < npatch - 1

    def convolve(act, weight, layer):
        col = lax.broadcasted_iota(jnp.int32, act.shape, 1)
        taps = jnp.concatenate([
            jnp.where(col == 0, 0.0, pltpu.roll(act, 1, 1)).astype(BF16),
            act.astype(BF16),
            jnp.where(col == tokens - 1, 0.0, pltpu.roll(act, tokens - 1, 1)).astype(BF16),
        ], axis=0)
        outer = dot(weight[0 : 2 * own, :], taps).astype(BF16)
        hsend[layer, 0] = outer[0:own]
        hsend[layer, 1] = outer[own : 2 * own]

        @pl.when(has_below)
        def _():
            hcopy(layer, 0).start()

        @pl.when(has_above)
        def _():
            hcopy(layer, 1).start()

        return dot(weight[2 * own : 3 * own, :], taps)

    def neighbours(layer):
        @pl.when(has_above)
        def _():
            hcopy(layer, 0).wait_recv()

        @pl.when(has_below)
        def _():
            hcopy(layer, 1).wait_recv()

        return hrecv[layer, 0].astype(F32) + hrecv[layer, 1].astype(F32)

    for layer in range(2):
        @pl.when(jnp.logical_not(has_above))
        def _():
            hrecv[layer, 0] = jnp.zeros((own, tokens), BF16)

        @pl.when(jnp.logical_not(has_below))
        def _():
            hrecv[layer, 1] = jnp.zeros((own, tokens), BF16)

    barrier = pltpu.get_barrier_semaphore()
    loop(1, everyone, lambda p: pl.semaphore_signal(
        barrier, inc=1, device_id=peer(p, 1), device_id_type=MESH))
    x1[mine, :] = latent[...]
    lat = latent[...].astype(F32)
    e16[...] = members((16, own), 0, own)
    et16[...] = members((own, 16), 1, own)
    stats(latent[...], 0)
    spread_w[...] = members(spread_w.shape, 1, own, 3)

    pl.semaphore_wait(barrier, everyone - 1)

    share(0)
    gx[0].start()
    L_T1.wait()
    hidden = silu(dot(emb[...], tw1[...]))
    L_TP.wait()
    bias = dot_nt(tpj[...], silu(hidden).astype(BF16))
    gx[0].forward()
    norm = combined(0, 1e-05)
    for load, g in zip((L_Q, L_K, L_V), gw):
        load.wait()
        g.start()
    gx[0].finish()
    L_PW.wait()
    gpw.start()
    for load in L_CONV[0]:
        load.wait()
    centre = convolve(silu(normalize(x1[...], norm)), cw1, 0)
    conv_one = (centre + neighbours(0) + bias[:, 0:1]).astype(BF16)
    x2[mine, :] = conv_one
    stats(conv_one, 1)

    share(1)
    gx[1].start()
    gpw.forward()
    gx[1].forward()
    norm = combined(1, 1e-05)
    gx[1].finish()
    L_OW.wait()
    gow.start()
    for load in L_CONV[1]:
        load.wait()
    centre = convolve(silu(normalize(x2[...], norm)), cw2, 1)
    resnet = (lat + (centre + neighbours(1))).astype(BF16)
    res[...] = resnet
    x3[mine, :] = resnet
    stats(resnet, 2)

    def zrow(to, source):
        ref = xr.at[source, mine]
        return pltpu.make_async_remote_copy(
            src_ref=ref, dst_ref=ref, send_sem=lnsend.at[to], recv_sem=lnrecv.at[source],
            device_id={"patch": to}, device_id_type=MESH,
        )

    def grow(source):
        return Gather(G_LN + source, xr.at[source], own)

    def nearest(rank):
        near = jnp.minimum(band, npatch - 1 - band)
        odd = rank % 2
        step = (rank + odd) // 2
        beyond = jnp.where(2 * band < npatch - 1, rank, npatch - 1 - rank)
        return jnp.where(rank <= 2 * near, band + (1 - 2 * odd) * step, beyond)

    share(2)
    gx[2].start()
    gow.forward()
    gx[2].forward()
    gpw.finish()
    for g in gw:
        if not aligned:
            g.forward()
        g.finish()
    norm = combined(2, 1e-06)
    gx[2].finish()

    head0 = (idx * own) // HEAD_DIM
    span = nheads * HEAD_DIM
    held = pl.ds(pl.multiple_of(head0 * HEAD_DIM, HEAD_DIM), span)

    projected = dot(pw[...], normalize(x3[...], norm).astype(BF16)).astype(BF16)
    proj[...] = projected
    wide = projected.astype(F32)
    wide = wide - jnp.mean(wide, axis=0, keepdims=True)
    spread = jnp.mean(wide * wide, axis=0, keepdims=True)
    xr[band] = (wide * lax.rsqrt(spread + 1e-05)).astype(BF16)
    loop(1, npatch, lambda r: zrow(nearest(r), band).start())

    def attend(normed, query, first):
        keys = dot(kw[held, :], normed).astype(BF16)
        values = dot(vw[held, :], normed).astype(BF16)
        for h in range(nheads):
            part = slice(h * HEAD_DIM, (h + 1) * HEAD_DIM)
            scores = dot_tn(keys[part], query[part])
            peak = jnp.max(scores, axis=0, keepdims=True)
            if not first:
                old = peaks[h]
                peak = jnp.maximum(peak, old)
                factor = jnp.exp(old - peak)
            weights = jnp.exp(scores - peak)
            total = jnp.sum(weights, axis=0, keepdims=True)
            update = dot(values[part], weights.astype(BF16))
            if not first:
                total = total + totals[h] * factor
                update = update + sums[part, :] * factor
            peaks[h] = peak
            totals[h] = total
            sums[part, :] = update

    def relay(rank):
        source = nearest(rank)
        zrow(source, source).wait_recv()
        grow(source).start()

    qry[...] = (dot(qw[held, :], xr[band]) * 0.125).astype(BF16)
    relay(1)
    attend(xr[band], qry[...], True)
    if npatch > 2:
        relay(2)
    grow(nearest(1)).forward()

    def arrive(rank):
        source = nearest(rank)
        grow(source).finish()
        attend(xr[source], qry[...], False)

    for rank in range(1, min(npatch, 3)):
        if rank + 2 < npatch:
            relay(rank + 2)
        if rank + 1 < npatch:
            grow(nearest(rank + 1)).forward()
        arrive(rank)

    def further(rank):
        if npatch > 4:
            @pl.when(rank + 2 < npatch)
            def _():
                relay(rank + 2)

            @pl.when(rank + 1 < npatch)
            def _():
                grow(nearest(rank + 1)).forward()
        arrive(rank)

    loop(3, npatch, further)
    for h in range(nheads):
        part = slice(h * HEAD_DIM, (h + 1) * HEAD_DIM)
        attn[part, :] = (sums[part, :] / totals[h]).astype(BF16)

    skip = pl.multiple_of(idx * own - head0 * HEAD_DIM, 16)
    at[mine, :] = attn[pl.ds(skip, own), :]
    gat.start()
    gat.forward()
    gow.finish()
    gat.finish()
    mixed = (proj[...].astype(F32) + dot(ow[...], at[...])).astype(BF16)
    L_PO.wait()
    out[...] = res[...].astype(F32) + dot(po[...], mixed)

    for g in gw + gx + [gpw, gow, gat]:
        g.drain()
    loop(1, npatch, lambda r: grow(nearest(r)).drain())
    loop(1, npatch, lambda r: zrow(nearest(r), band).wait_send())
    for layer in range(3):
        loop(1, everyone, lambda p: zcopy(layer, p).wait_send())
    for layer in range(2):
        @pl.when(has_below)
        def _():
            hcopy(layer, 0).wait_send()

        @pl.when(has_above)
        def _():
            hcopy(layer, 1).wait_send()


def local(
    npatch, nchan, nsub,
    latent, timestep, time_w1, time_proj, conv1_w, conv2_w, proj_in_w, q_w, kv_w, out_w, proj_out_w,
):
    own, tokens = latent.shape
    nheads = -(-own // HEAD_DIM)
    nidx = nchan * nsub
    temb = time_w1.shape[0]
    half_width = FREQ // 2
    place = lax.broadcasted_iota(jnp.int32, (16, FREQ), 1)
    first = place < half_width
    order = jnp.where(first, place, place - half_width).astype(F32)
    angles = timestep[0].astype(F32) * jnp.exp(-math.log(10000.0) * order / half_width)
    emb = jnp.where(first, jnp.cos(angles), jnp.sin(angles)).astype(BF16)
    vmem = pl.BlockSpec(memory_space=pltpu.VMEM)
    hbm = pl.BlockSpec(memory_space=pl.ANY)
    dma = pltpu.SemaphoreType.DMA
    span = nheads * HEAD_DIM
    ngather = G_LN + npatch
    total = pl.pallas_call(
        functools.partial(kernel, npatch, nchan, nsub, own, nheads),
        out_shape=jax.ShapeDtypeStruct((own, tokens), F32),
        in_specs=[vmem, vmem] + [hbm] * 9,
        out_specs=vmem,
        scratch_shapes=[
            pltpu.VMEM((FREQ, temb), BF16),
            pltpu.VMEM((own, temb), BF16),
            pltpu.VMEM((3 * own, 3 * C), BF16),
            pltpu.VMEM((3 * own, 3 * C), BF16),
            pltpu.VMEM((own, C), BF16),
        ]
        + [pltpu.VMEM((C, C), BF16)] * 5
        + [pltpu.VMEM((C, tokens), BF16)] * 4
        + [
            pltpu.VMEM((16, own), BF16),
            pltpu.VMEM((own, 16), BF16),
            pltpu.VMEM((C, 3 * nidx * 8), BF16),
        ]
        + [
            pltpu.VMEM((3, npatch, nidx * 8, 128), F32),
            pltpu.VMEM((2, 2, own, tokens), BF16),
            pltpu.VMEM((2, 2, own, tokens), BF16),
            pltpu.VMEM((npatch, C, tokens), BF16),
            pltpu.VMEM((span, tokens), BF16),
            pltpu.VMEM((nheads, 1, tokens), F32),
            pltpu.VMEM((nheads, 1, tokens), F32),
            pltpu.VMEM((span, tokens), F32),
            pltpu.VMEM((span, tokens), BF16),
            pltpu.VMEM((C, tokens), BF16),
            pltpu.VMEM((own, tokens), BF16),
            dma((26,)),
            dma((ngather, nchan, nsub)),
            dma((ngather, nchan, nsub)),
            dma((3, npatch * nidx)),
            dma((3, npatch * nidx)),
            dma((2, 2)),
            dma((2, 2)),
            dma((npatch,)),
            dma((npatch,)),
        ],
        compiler_params=pltpu.CompilerParams(
            collective_id=0, has_side_effects=True, vmem_limit_bytes=60 * 1024 * 1024
        ),
    )(
        latent, emb, time_w1.T, time_proj, conv1_w, conv2_w, proj_in_w, q_w, kv_w, out_w, proj_out_w
    )
    return total.astype(BF16)


def solution(mesh):
    in_specs = (
        P(("chan", "sub"), ("groups", "patch")),
        P("groups"),
        P(),
        P(("chan", "sub"), None),
        P(None, ("chan", "sub"), None),
        P(None, ("chan", "sub"), None),
        P(("chan", "sub"), None),
        P(("chan", "sub"), None),
        P(None, ("chan", "sub"), None),
        P(("chan", "sub"), None),
        P(("chan", "sub"), None),
    )
    out_specs = P(("chan", "sub"), ("groups", "patch"))
    sizes = [mesh.shape[a] for a in ("patch", "chan", "sub")]
    return jax.shard_map(
        functools.partial(local, *sizes), mesh=mesh, in_specs=in_specs, out_specs=out_specs, check_vma=False
    )
```

```python
import functools
import math

import jax
import jax.numpy as jnp
from jax import lax
from jax.experimental import pallas as pl
from jax.experimental.pallas import tpu as pltpu
from jax.sharding import PartitionSpec as P

C = 640
HEADS = 10
HEAD_DIM = 64
NGROUPS = 32
FREQ = 320
WIDTH = 256
GROUP = C // NGROUPS
MESH = pl.DeviceIdType.MESH
F32 = jnp.float32
BF16 = jnp.bfloat16
HIGH = lax.Precision.HIGHEST

G_PW, G_OW, G_Q, G_K, G_V, G_X1, G_X2, G_X3, G_AT = range(9)
G_LN = 9


def dot(a, b, precision=None):
    return jnp.dot(a, b, preferred_element_type=F32, precision=precision)


def dot_nt(a, b):
    return lax.dot_general(a, b, (((1,), (1,)), ((), ())), preferred_element_type=F32)


def dot_tn(a, b):
    return lax.dot_general(a, b, (((0,), (0,)), ((), ())), preferred_element_type=F32)


def loop(low, high, body):
    if high - low <= 16:
        for k in range(low, high):
            body(k)
    else:
        lax.fori_loop(low, high, lambda k, _: (body(k), 0)[1], 0)


def silu(v):
    half = 0.5 * v
    return half + half * jnp.tanh(half)


def kernel(
    npatch, nchan, nsub, own, nheads,
    latent_hbm, emb_hbm, time_w1, time_proj, conv1_w, conv2_w, proj_in_w, q_w, kv_w, out_w, proj_out_w,
    out,
    emb, tw1, tpj, cw1, cw2, po, pw, ow, qw, kw, vw, x1, x2, x3, at, e16, et16, spread_w, zst, hsend, hrecv,
    xr, vals, scores, attn, proj, res,
    lsem, gsend, grecv, zsend, zrecv, hssem, hrsem, lnsend, lnrecv,
):
    band = lax.axis_index("patch")
    chan = lax.axis_index("chan")
    sub = lax.axis_index("sub")
    idx = chan * nsub + sub
    nidx = nchan * nsub
    tokens = x1.shape[1]
    aligned = (own * nsub) % HEAD_DIM == 0

    def rows(block, size):
        return pl.ds(pl.multiple_of(block * size, 16 if size % 16 == 0 else 8), size)

    mine = rows(idx, own)
    pairs = [
        (time_w1, tw1), (time_proj, tpj), (q_w, qw.at[mine]), (kv_w.at[0], kw.at[mine]),
        (kv_w.at[1], vw.at[mine]), (proj_in_w, pw.at[mine]), (out_w, ow.at[mine]), (proj_out_w, po),
    ]
    pairs += [(conv1_w, cw1), (conv2_w, cw2), (latent_hbm, x1.at[mine]), (emb_hbm, emb)]
    loads = [pltpu.make_async_copy(a, b, lsem.at[i]) for i, (a, b) in enumerate(pairs)]
    L_T1, L_TP, L_Q, L_K, L_V, L_PW, L_OW, L_PO = loads[:8]
    L_C1, L_C2, L_X, L_E = loads[8:]
    for load in (L_X, L_E, L_T1, L_TP, L_C1, L_Q, L_K, L_V, L_PW, L_C2, L_OW, L_PO):
        load.start()

    def other(k, by, count):
        to = k + by + count
        to = jnp.where(to >= 2 * count, to - 2 * count, to)
        return jnp.where(to >= count, to - count, to)

    class Gather:
        def __init__(self, g, buf, size, only_sub=False):
            self.g, self.buf, self.size = g, buf, size
            self.chans = 1 if only_sub else nchan

        def copy(self, block, d, s):
            ref = self.buf.at[rows(block, self.size)]
            to = {"chan": other(chan, d, nchan)} if s == 0 else {"sub": other(sub, s, nsub)}
            return pltpu.make_async_remote_copy(
                src_ref=ref, dst_ref=ref, send_sem=gsend.at[self.g, d, s],
                recv_sem=grecv.at[self.g, d, s], device_id=to, device_id_type=MESH,
            )

        def start(self):
            for d in range(1, self.chans):
                self.copy(idx, d, 0).start()
            for s in range(1, nsub):
                self.copy(idx, 0, s).start()

        def forward(self):
            for d in range(1, self.chans):
                block = other(chan, -d, nchan) * nsub + sub
                self.copy(block, d, 0).wait_recv()
                for s in range(1, nsub):
                    self.copy(block, d, s).start()

        def finish(self):
            for d in range(self.chans):
                for s in range(1, nsub):
                    block = other(chan, -d, nchan) * nsub + other(sub, -s, nsub)
                    self.copy(block, d, s).wait_recv()

        def drain(self):
            for d in range(self.chans):
                for s in range(nsub):
                    if d or s:
                        self.copy(idx, d, s).wait_send()

    gw = [
        Gather(G_Q, qw, own, aligned), Gather(G_K, kw, own, aligned), Gather(G_V, vw, own, aligned),
    ]
    gpw, gow = Gather(G_PW, pw, own), Gather(G_OW, ow, own)
    gx = [Gather(G_X1, x1, own), Gather(G_X2, x2, own), Gather(G_X3, x3, own)]
    gat = Gather(G_AT, at, own)

    cell = GROUP * tokens

    def members(shape, group_dim, size, times=1):
        gi = lax.broadcasted_iota(jnp.int32, shape, group_dim)
        ci = lax.broadcasted_iota(jnp.int32, shape, 1 - group_dim)
        period = shape[group_dim] // times
        for k in range(times - 1, 0, -1):
            gi = jnp.where(gi >= k * period, gi - k * period, gi)
        g = gi & 7
        first = (gi >> 3) * size + g * GROUP
        inside = (ci >= first) & (ci < first + GROUP) & (g < size // GROUP)
        return jnp.where(inside, 1.0, 0.0).astype(BF16)

    def stats(x, layer):
        mean = jnp.sum(dot(e16[...], x), axis=1, keepdims=True) * (1.0 / cell)
        mean = jnp.broadcast_to(mean, (16, 128))
        shift = mean.astype(BF16)
        sc = dot(et16[...], shift)
        sq = jnp.zeros((own, 128), F32)
        for k in range(0, tokens, 128):
            dev = x[:, k : k + 128].astype(F32) - sc
            sq = sq + dev * dev
        hi = sq.astype(BF16)
        lo = (sq - hi.astype(F32)).astype(BF16)
        m2 = jnp.sum(dot(e16[...], jnp.concatenate([hi, lo], axis=1)), axis=1, keepdims=True)
        gap = mean - shift.astype(F32)
        m2 = jnp.maximum(m2 - cell * (gap * gap), 0.0)
        lane = lax.broadcasted_iota(jnp.int32, (16, 128), 1)
        zst[layer, band, rows(idx, 8)] = jnp.where(lane < 64, mean, m2)[0:8]

    everyone = npatch * nidx

    def peer(p, way):
        k = p % nidx
        return {
            "patch": other(band, way * (p // nidx), npatch),
            "chan": other(chan, way * (k // nsub), nchan),
            "sub": other(sub, way * (k % nsub), nsub),
        }

    def zcopy(layer, p, source=None):
        b, k = (band, idx) if source is None else (source["patch"], source["chan"] * nsub + source["sub"])
        ref = zst.at[layer, b, rows(k, 8)]
        return pltpu.make_async_remote_copy(
            src_ref=ref, dst_ref=ref, send_sem=zsend.at[layer, p], recv_sem=zrecv.at[layer, p],
            device_id=peer(p, 1), device_id_type=MESH,
        )

    def share(layer):
        loop(1, everyone, lambda p: zcopy(layer, p).start())

    def combined(layer, eps):
        loop(1, everyone, lambda p: zcopy(layer, p, peer(p, -1)).wait_recv())
        tile = zst[layer]
        means, m2s = tile[:, :, 0:1], tile[:, :, 127:128]
        mean = jnp.sum(means, axis=0) * (1.0 / npatch)
        dev = means - mean[None]
        var = jnp.sum(m2s + cell * (dev * dev), axis=0) * (1.0 / (cell * npatch))
        shape = (nidx * 8, 128)
        lane = lax.broadcasted_iota(jnp.int32, shape, 1)
        pair = jnp.where(
            lane < 64, jnp.broadcast_to(mean, shape), jnp.broadcast_to(lax.rsqrt(var + eps), shape)
        )
        one = pair.astype(BF16)
        rest = pair - one.astype(F32)
        two = rest.astype(BF16)
        three = (rest - two.astype(F32)).astype(BF16)
        return dot(spread_w[...], jnp.concatenate([one, two, three], axis=0))

    def normalize(x, both):
        return (x.astype(F32) - both[:, 0:1]) * both[:, 64:65]

    def hcopy(layer, way):
        return pltpu.make_async_remote_copy(
            src_ref=hsend.at[layer, way], dst_ref=hrecv.at[layer, way],
            send_sem=hssem.at[layer, way], recv_sem=hrsem.at[layer, way],
            device_id={"patch": other(band, 1 - 2 * way, npatch)}, device_id_type=MESH,
        )

    has_above, has_below = band > 0, band < npatch - 1

    def convolve(act, weight, layer):
        col = lax.broadcasted_iota(jnp.int32, act.shape, 1)
        taps = [
            jnp.where(col == 0, 0.0, pltpu.roll(act, 1, 1)).astype(BF16),
            act.astype(BF16),
            jnp.where(col == tokens - 1, 0.0, pltpu.roll(act, tokens - 1, 1)).astype(BF16),
        ]

        def row(i):
            return sum(dot(weight[3 * i + j], taps[j]) for j in range(3))

        hsend[layer, 0] = row(0).astype(BF16)

        @pl.when(has_below)
        def _():
            hcopy(layer, 0).start()

        hsend[layer, 1] = row(2).astype(BF16)

        @pl.when(has_above)
        def _():
            hcopy(layer, 1).start()

        return row(1)

    def neighbours(layer):
        @pl.when(has_above)
        def _():
            hcopy(layer, 0).wait_recv()

        @pl.when(has_below)
        def _():
            hcopy(layer, 1).wait_recv()

        return hrecv[layer, 0].astype(F32) + hrecv[layer, 1].astype(F32)

    for layer in range(2):
        @pl.when(jnp.logical_not(has_above))
        def _():
            hrecv[layer, 0] = jnp.zeros((own, tokens), BF16)

        @pl.when(jnp.logical_not(has_below))
        def _():
            hrecv[layer, 1] = jnp.zeros((own, tokens), BF16)

    barrier = pltpu.get_barrier_semaphore()
    loop(1, everyone, lambda p: pl.semaphore_signal(
        barrier, inc=1, device_id=peer(p, 1), device_id_type=MESH))
    e16[...] = members((16, own), 0, own)
    et16[...] = members((own, 16), 1, own)
    L_X.wait()
    stats(x1[mine, :], 0)
    spread_w[...] = members(spread_w.shape, 1, own, 3)

    pl.semaphore_wait(barrier, everyone - 1)

    share(0)
    gx[0].start()
    L_T1.wait()
    L_E.wait()
    hidden = silu(dot(emb[...], tw1[...]))
    L_TP.wait()
    bias = dot_nt(tpj[...], silu(hidden).astype(BF16))
    gx[0].forward()
    norm = combined(0, 1e-05)
    for load, g in zip((L_Q, L_K, L_V), gw):
        load.wait()
        g.start()
    gx[0].finish()
    L_PW.wait()
    gpw.start()
    L_C1.wait()
    centre = convolve(silu(normalize(x1[...], norm)), cw1, 0)
    conv_one = (centre + neighbours(0) + bias[:, 0:1]).astype(BF16)
    x2[mine, :] = conv_one
    stats(conv_one, 1)

    share(1)
    gx[1].start()
    gpw.forward()
    gx[1].forward()
    norm = combined(1, 1e-05)
    gx[1].finish()
    L_OW.wait()
    gow.start()
    L_C2.wait()
    centre = convolve(silu(normalize(x2[...], norm)), cw2, 1)
    resnet = (x1[mine, :].astype(F32) + (centre + neighbours(1))).astype(BF16)
    res[...] = resnet
    x3[mine, :] = resnet
    stats(resnet, 2)

    def zrow(to, source):
        ref = xr.at[source, mine]
        return pltpu.make_async_remote_copy(
            src_ref=ref, dst_ref=ref, send_sem=lnsend.at[to], recv_sem=lnrecv.at[source],
            device_id={"patch": to}, device_id_type=MESH,
        )

    def grow(source):
        return Gather(G_LN + source, xr.at[source], own)

    def nearest(rank):
        near = jnp.minimum(band, npatch - 1 - band)
        odd = rank % 2
        step = (rank + odd) // 2
        beyond = jnp.where(2 * band < npatch - 1, rank, npatch - 1 - rank)
        return jnp.where(rank <= 2 * near, band + (1 - 2 * odd) * step, beyond)

    share(2)
    gx[2].start()
    gow.forward()
    gx[2].forward()
    gpw.finish()
    for g in gw:
        if not aligned:
            g.forward()
        g.finish()
    norm = combined(2, 1e-06)
    gx[2].finish()

    head0 = (idx * own) // HEAD_DIM
    span = nheads * HEAD_DIM
    held = pl.ds(pl.multiple_of(head0 * HEAD_DIM, HEAD_DIM), span)

    projected = dot(pw[...], normalize(x3[...], norm).astype(BF16)).astype(BF16)
    proj[...] = projected
    wide = projected.astype(F32)
    wide = wide - jnp.mean(wide, axis=0, keepdims=True)
    spread = jnp.mean(wide * wide, axis=0, keepdims=True)
    xr[band] = (wide * lax.rsqrt(spread + 1e-05)).astype(BF16)
    loop(1, npatch, lambda r: zrow(nearest(r), band).start())

    def score(source):
        normed = xr[source]
        keys = dot(kw[held, :], normed).astype(BF16)
        vals[source] = dot(vw[held, :], normed).astype(BF16)
        for h in range(nheads):
            part = slice(h * HEAD_DIM, (h + 1) * HEAD_DIM)
            scores[source, h] = dot_tn(keys[part], query[part])

    def relay(rank):
        source = nearest(rank)
        zrow(source, source).wait_recv()
        grow(source).start()

    query = (dot(qw[held, :], xr[band]) * 0.125).astype(BF16)
    score(band)
    relay(1)

    def pass_on(rank):
        relay(rank)
        grow(nearest(rank - 1)).forward()

    loop(2, npatch, pass_on)
    grow(nearest(npatch - 1)).forward()

    def arrive(rank):
        source = nearest(rank)
        grow(source).finish()
        score(source)

    loop(1, npatch, arrive)

    for h in range(nheads):
        part = slice(h * HEAD_DIM, (h + 1) * HEAD_DIM)

        def peak_of(b, peak):
            return jnp.maximum(peak, jnp.max(scores[b, h], axis=0, keepdims=True))

        def add(b, so_far):
            total, weighted = so_far
            weights = jnp.exp(scores[b, h] - peak)
            total = total + jnp.sum(weights, axis=0, keepdims=True)
            return total, weighted + dot(vals[b, part], weights.astype(BF16))

        peak = jnp.full((1, tokens), -jnp.inf, F32)
        so_far = (jnp.zeros((1, tokens), F32), jnp.zeros((HEAD_DIM, tokens), F32))
        if npatch <= 4:
            for b in range(npatch):
                peak = peak_of(b, peak)
            for b in range(npatch):
                so_far = add(b, so_far)
        else:
            peak = lax.fori_loop(0, npatch, peak_of, peak)
            so_far = lax.fori_loop(0, npatch, add, so_far)
        attn[part, :] = (so_far[1] / so_far[0]).astype(BF16)

    skip = pl.multiple_of(idx * own - head0 * HEAD_DIM, 16)
    at[mine, :] = attn[pl.ds(skip, own), :]
    gat.start()
    gat.forward()
    gow.finish()
    gat.finish()
    mixed = (proj[...].astype(F32) + dot(ow[...], at[...])).astype(BF16)
    L_PO.wait()
    out[...] = res[...].astype(F32) + dot(po[...], mixed)

    for g in gw + gx + [gpw, gow, gat]:
        g.drain()
    loop(1, npatch, lambda r: grow(nearest(r)).drain())
    loop(1, npatch, lambda r: zrow(nearest(r), band).wait_send())
    for layer in range(3):
        loop(1, everyone, lambda p: zcopy(layer, p).wait_send())
    for layer in range(2):
        @pl.when(has_below)
        def _():
            hcopy(layer, 0).wait_send()

        @pl.when(has_above)
        def _():
            hcopy(layer, 1).wait_send()


def local(
    npatch, nchan, nsub,
    latent, timestep, time_w1, time_proj, conv1_w, conv2_w, proj_in_w, q_w, kv_w, out_w, proj_out_w,
):
    own, tokens = latent.shape
    nheads = -(-own // HEAD_DIM)
    nidx = nchan * nsub
    temb = time_w1.shape[0]
    half_width = FREQ // 2
    place = lax.broadcasted_iota(jnp.int32, (16, FREQ), 1)
    first = place < half_width
    order = jnp.where(first, place, place - half_width).astype(F32)
    angles = timestep[0].astype(F32) * jnp.exp(-math.log(10000.0) * order / half_width)
    emb = jnp.where(first, jnp.cos(angles), jnp.sin(angles)).astype(BF16)
    vmem = pl.BlockSpec(memory_space=pltpu.VMEM)
    hbm = pl.BlockSpec(memory_space=pl.ANY)
    dma = pltpu.SemaphoreType.DMA
    span = nheads * HEAD_DIM
    ngather = G_LN + npatch
    total = pl.pallas_call(
        functools.partial(kernel, npatch, nchan, nsub, own, nheads),
        out_shape=pltpu.VMEM((own, tokens), F32),
        in_specs=[hbm] * 11,
        out_specs=vmem,
        scratch_shapes=[
            pltpu.VMEM((16, FREQ), BF16),
            pltpu.VMEM((FREQ, temb), BF16),
            pltpu.VMEM((own, temb), BF16),
            pltpu.VMEM((9, own, C), BF16),
            pltpu.VMEM((9, own, C), BF16),
            pltpu.VMEM((own, C), BF16),
        ]
        + [pltpu.VMEM((C, C), BF16)] * 5
        + [pltpu.VMEM((C, tokens), BF16)] * 4
        + [
            pltpu.VMEM((16, own), BF16),
            pltpu.VMEM((own, 16), BF16),
            pltpu.VMEM((C, 3 * nidx * 8), BF16),
        ]
        + [
            pltpu.VMEM((3, npatch, nidx * 8, 128), F32),
            pltpu.VMEM((2, 2, own, tokens), BF16),
            pltpu.VMEM((2, 2, own, tokens), BF16),
            pltpu.VMEM((npatch, C, tokens), BF16),
            pltpu.VMEM((npatch, span, tokens), BF16),
            pltpu.VMEM((npatch, nheads, tokens, tokens), F32),
            pltpu.VMEM((span, tokens), BF16),
            pltpu.VMEM((C, tokens), BF16),
            pltpu.VMEM((own, tokens), BF16),
            dma((12,)),
            dma((ngather, nchan, nsub)),
            dma((ngather, nchan, nsub)),
            dma((3, npatch * nidx)),
            dma((3, npatch * nidx)),
            dma((2, 2)),
            dma((2, 2)),
            dma((npatch,)),
            dma((npatch,)),
        ],
        compiler_params=pltpu.CompilerParams(
            collective_id=0, has_side_effects=True, vmem_limit_bytes=60 * 1024 * 1024
        ),
    )(
        latent, emb, time_w1.T, time_proj, conv1_w, conv2_w, proj_in_w, q_w, kv_w, out_w, proj_out_w
    )
    return total.astype(BF16)


def solution(mesh):
    in_specs = (
        P(("chan", "sub"), ("groups", "patch")),
        P("groups"),
        P(),
        P(("chan", "sub"), None),
        P(None, ("chan", "sub"), None),
        P(None, ("chan", "sub"), None),
        P(("chan", "sub"), None),
        P(("chan", "sub"), None),
        P(None, ("chan", "sub"), None),
        P(("chan", "sub"), None),
        P(("chan", "sub"), None),
    )
    out_specs = P(("chan", "sub"), ("groups", "patch"))
    sizes = [mesh.shape[a] for a in ("patch", "chan", "sub")]
    return jax.shard_map(
        functools.partial(local, *sizes), mesh=mesh, in_specs=in_specs, out_specs=out_specs, check_vma=False
    )
```

```python
import functools
import math

import jax
import jax.numpy as jnp
from jax import lax
from jax.experimental import pallas as pl
from jax.experimental.pallas import tpu as pltpu
from jax.sharding import PartitionSpec as P

C = 640
HEADS = 10
HEAD_DIM = 64
NGROUPS = 32
FREQ = 320
WIDTH = 256
GROUP = C // NGROUPS
MESH = pl.DeviceIdType.MESH
F32 = jnp.float32
BF16 = jnp.bfloat16
HIGH = lax.Precision.HIGHEST

G_PW, G_OW, G_Q, G_K, G_V, G_X1, G_X2, G_AT = range(8)
G_LN = 8


def dot(a, b, precision=None):
    return jnp.dot(a, b, preferred_element_type=F32, precision=precision)


def dot_nt(a, b):
    return lax.dot_general(a, b, (((1,), (1,)), ((), ())), preferred_element_type=F32)


def dot_tn(a, b):
    return lax.dot_general(a, b, (((0,), (0,)), ((), ())), preferred_element_type=F32)


def loop(low, high, body):
    if high - low <= 16:
        for k in range(low, high):
            body(k)
    else:
        lax.fori_loop(low, high, lambda k, _: (body(k), 0)[1], 0)


def silu(v):
    half = 0.5 * v
    return half + half * jnp.tanh(half)


def kernel(
    npatch, nchan, nsub, own, nheads,
    latent_hbm, emb_hbm, time_w1, time_proj, conv1_w, conv2_w, proj_in_w, q_w, kv_w, out_w, proj_out_w,
    out,
    emb, tw1, tpj, cw1, cw2, po, pw, ow, qw, kw, vw, x1, x2, nmean, nscale, at, e16, et16, spread_w, zst, hsend, hrecv,
    xr, vals, scores, attn, proj, res,
    lsem, gsend, grecv, zsend, zrecv, hssem, hrsem, lnsend, lnrecv,
):
    band = lax.axis_index("patch")
    chan = lax.axis_index("chan")
    sub = lax.axis_index("sub")
    idx = chan * nsub + sub
    nidx = nchan * nsub
    tokens = x1.shape[1]
    aligned = (own * nsub) % HEAD_DIM == 0

    def rows(block, size):
        return pl.ds(pl.multiple_of(block * size, 16 if size % 16 == 0 else 8), size)

    mine = rows(idx, own)
    pairs = [
        (time_w1, tw1), (time_proj, tpj), (q_w, qw.at[mine]), (kv_w.at[0], kw.at[mine]),
        (kv_w.at[1], vw.at[mine]), (proj_in_w, pw.at[mine]), (out_w, ow.at[mine]), (proj_out_w, po),
    ]
    pairs += [(conv1_w, cw1), (conv2_w, cw2), (latent_hbm, x1.at[mine]), (emb_hbm, emb)]
    loads = [pltpu.make_async_copy(a, b, lsem.at[i]) for i, (a, b) in enumerate(pairs)]
    L_T1, L_TP, L_Q, L_K, L_V, L_PW, L_OW, L_PO = loads[:8]
    L_C1, L_C2, L_X, L_E = loads[8:]
    for load in (L_X, L_E, L_T1, L_TP, L_C1, L_Q, L_K, L_V, L_PW, L_C2, L_OW, L_PO):
        load.start()

    def other(k, by, count):
        to = k + by + count
        to = jnp.where(to >= 2 * count, to - 2 * count, to)
        return jnp.where(to >= count, to - count, to)

    class Gather:
        def __init__(self, g, buf, size, only_sub=False):
            self.g, self.buf, self.size = g, buf, size
            self.chans = 1 if only_sub else nchan

        def copy(self, block, d, s):
            ref = self.buf.at[rows(block, self.size)]
            to = {"chan": other(chan, d, nchan)} if s == 0 else {"sub": other(sub, s, nsub)}
            return pltpu.make_async_remote_copy(
                src_ref=ref, dst_ref=ref, send_sem=gsend.at[self.g, d, s],
                recv_sem=grecv.at[self.g, d, s], device_id=to, device_id_type=MESH,
            )

        def start(self):
            for d in range(1, self.chans):
                self.copy(idx, d, 0).start()
            for s in range(1, nsub):
                self.copy(idx, 0, s).start()

        def forward(self):
            for d in range(1, self.chans):
                block = other(chan, -d, nchan) * nsub + sub
                self.copy(block, d, 0).wait_recv()
                for s in range(1, nsub):
                    self.copy(block, d, s).start()

        def finish(self):
            for d in range(self.chans):
                for s in range(1, nsub):
                    block = other(chan, -d, nchan) * nsub + other(sub, -s, nsub)
                    self.copy(block, d, s).wait_recv()

        def drain(self):
            for d in range(self.chans):
                for s in range(nsub):
                    if d or s:
                        self.copy(idx, d, s).wait_send()

    gw = [
        Gather(G_Q, qw, own, aligned), Gather(G_K, kw, own, aligned), Gather(G_V, vw, own, aligned),
    ]
    gpw, gow = Gather(G_PW, pw, own), Gather(G_OW, ow, own)
    gx = [Gather(G_X1, x1, own), Gather(G_X2, x2, own)]
    gat = Gather(G_AT, at, own)

    cell = GROUP * tokens

    def members(shape, group_dim, size, times=1):
        gi = lax.broadcasted_iota(jnp.int32, shape, group_dim)
        ci = lax.broadcasted_iota(jnp.int32, shape, 1 - group_dim)
        period = shape[group_dim] // times
        for k in range(times - 1, 0, -1):
            gi = jnp.where(gi >= k * period, gi - k * period, gi)
        g = gi & 7
        first = (gi >> 3) * size + g * GROUP
        inside = (ci >= first) & (ci < first + GROUP) & (g < size // GROUP)
        return jnp.where(inside, 1.0, 0.0).astype(BF16)

    def stats(x, layer):
        mean = jnp.sum(dot(e16[...], x), axis=1, keepdims=True) * (1.0 / cell)
        mean = jnp.broadcast_to(mean, (16, 128))
        shift = mean.astype(BF16)
        sc = dot(et16[...], shift)
        sq = jnp.zeros((own, 128), F32)
        for k in range(0, tokens, 128):
            dev = x[:, k : k + 128].astype(F32) - sc
            sq = sq + dev * dev
        hi = sq.astype(BF16)
        lo = (sq - hi.astype(F32)).astype(BF16)
        m2 = jnp.sum(dot(e16[...], jnp.concatenate([hi, lo], axis=1)), axis=1, keepdims=True)
        gap = mean - shift.astype(F32)
        m2 = jnp.maximum(m2 - cell * (gap * gap), 0.0)
        lane = lax.broadcasted_iota(jnp.int32, (16, 128), 1)
        zst[layer, band, rows(idx, 8)] = jnp.where(lane < 64, mean, m2)[0:8]

    everyone = npatch * nidx

    def peer(p, way):
        k = p % nidx
        return {
            "patch": other(band, way * (p // nidx), npatch),
            "chan": other(chan, way * (k // nsub), nchan),
            "sub": other(sub, way * (k % nsub), nsub),
        }

    def zcopy(layer, p, source=None):
        b, k = (band, idx) if source is None else (source["patch"], source["chan"] * nsub + source["sub"])
        ref = zst.at[layer, b, rows(k, 8)]
        return pltpu.make_async_remote_copy(
            src_ref=ref, dst_ref=ref, send_sem=zsend.at[layer, p], recv_sem=zrecv.at[layer, p],
            device_id=peer(p, 1), device_id_type=MESH,
        )

    def share(layer):
        loop(1, everyone, lambda p: zcopy(layer, p).start())

    def combined(layer, eps):
        loop(1, everyone, lambda p: zcopy(layer, p, peer(p, -1)).wait_recv())
        tile = zst[layer]
        means, m2s = tile[:, :, 0:1], tile[:, :, 127:128]
        mean = jnp.sum(means, axis=0) * (1.0 / npatch)
        dev = means - mean[None]
        var = jnp.sum(m2s + cell * (dev * dev), axis=0) * (1.0 / (cell * npatch))
        shape = (nidx * 8, 128)
        lane = lax.broadcasted_iota(jnp.int32, shape, 1)
        pair = jnp.where(
            lane < 64, jnp.broadcast_to(mean, shape), jnp.broadcast_to(lax.rsqrt(var + eps), shape)
        )
        one = pair.astype(BF16)
        rest = pair - one.astype(F32)
        two = rest.astype(BF16)
        three = (rest - two.astype(F32)).astype(BF16)
        return dot(spread_w[...], jnp.concatenate([one, two, three], axis=0))

    def normalize(x, both):
        return (x.astype(F32) - both[:, 0:1]) * both[:, 64:65]

    def hcopy(layer, way):
        return pltpu.make_async_remote_copy(
            src_ref=hsend.at[layer, way], dst_ref=hrecv.at[layer, way],
            send_sem=hssem.at[layer, way], recv_sem=hrsem.at[layer, way],
            device_id={"patch": other(band, 1 - 2 * way, npatch)}, device_id_type=MESH,
        )

    has_above, has_below = band > 0, band < npatch - 1

    def convolve(act, weight, layer):
        col = lax.broadcasted_iota(jnp.int32, act.shape, 1)
        taps = [
            jnp.where(col == 0, 0.0, pltpu.roll(act, 1, 1)).astype(BF16),
            act.astype(BF16),
            jnp.where(col == tokens - 1, 0.0, pltpu.roll(act, tokens - 1, 1)).astype(BF16),
        ]

        def row(i):
            return sum(dot(weight[3 * i + j], taps[j]) for j in range(3))

        hsend[layer, 0] = row(0).astype(BF16)

        @pl.when(has_below)
        def _():
            hcopy(layer, 0).start()

        hsend[layer, 1] = row(2).astype(BF16)

        @pl.when(has_above)
        def _():
            hcopy(layer, 1).start()

        return row(1)

    def neighbours(layer):
        @pl.when(has_above)
        def _():
            hcopy(layer, 0).wait_recv()

        @pl.when(has_below)
        def _():
            hcopy(layer, 1).wait_recv()

        return hrecv[layer, 0].astype(F32) + hrecv[layer, 1].astype(F32)

    for layer in range(2):
        @pl.when(jnp.logical_not(has_above))
        def _():
            hrecv[layer, 0] = jnp.zeros((own, tokens), BF16)

        @pl.when(jnp.logical_not(has_below))
        def _():
            hrecv[layer, 1] = jnp.zeros((own, tokens), BF16)

    barrier = pltpu.get_barrier_semaphore()
    loop(1, everyone, lambda p: pl.semaphore_signal(
        barrier, inc=1, device_id=peer(p, 1), device_id_type=MESH))
    e16[...] = members((16, own), 0, own)
    et16[...] = members((own, 16), 1, own)
    L_X.wait()
    stats(x1[mine, :], 0)
    spread_w[...] = members(spread_w.shape, 1, own, 3)

    pl.semaphore_wait(barrier, everyone - 1)

    share(0)
    gx[0].start()
    L_T1.wait()
    L_E.wait()
    hidden = silu(dot(emb[...], tw1[...]))
    L_TP.wait()
    bias = dot_nt(tpj[...], silu(hidden).astype(BF16))
    gx[0].forward()
    norm = combined(0, 1e-05)
    for load, g in zip((L_Q, L_K, L_V), gw):
        load.wait()
        g.start()
    gx[0].finish()
    L_PW.wait()
    gpw.start()
    L_C1.wait()
    centre = convolve(silu(normalize(x1[...], norm)), cw1, 0)
    conv_one = (centre + neighbours(0) + bias[:, 0:1]).astype(BF16)
    x2[mine, :] = conv_one
    stats(conv_one, 1)

    share(1)
    gx[1].start()
    gpw.forward()
    gx[1].forward()
    norm = combined(1, 1e-05)
    gx[1].finish()
    L_OW.wait()
    gow.start()
    L_C2.wait()
    centre = convolve(silu(normalize(x2[...], norm)), cw2, 1)
    resnet = (x1[mine, :].astype(F32) + (centre + neighbours(1))).astype(BF16)
    res[...] = resnet
    xr[band, mine, :] = resnet

    def zrow(to, source):
        ref = xr.at[source, mine]
        return pltpu.make_async_remote_copy(
            src_ref=ref, dst_ref=ref, send_sem=lnsend.at[to], recv_sem=lnrecv.at[source],
            device_id={"patch": to}, device_id_type=MESH,
        )

    def grow(source):
        return Gather(G_LN + source, xr.at[source], own)

    def nearest(rank):
        near = jnp.minimum(band, npatch - 1 - band)
        odd = rank % 2
        step = (rank + odd) // 2
        beyond = jnp.where(2 * band < npatch - 1, rank, npatch - 1 - rank)
        return jnp.where(rank <= 2 * near, band + (1 - 2 * odd) * step, beyond)

    loop(1, npatch, lambda r: zrow(nearest(r), band).start())
    grow(band).start()
    stats(resnet, 2)
    share(2)
    grow(band).forward()

    def relay(rank):
        source = nearest(rank)
        zrow(source, source).wait_recv()
        grow(source).start()

    gow.forward()
    gpw.finish()
    for g in gw:
        if not aligned:
            g.forward()
        g.finish()
    relay(1)
    norm = combined(2, 1e-06)
    nmean[...] = jnp.broadcast_to(norm[:, 0:1], (C, 128))
    nscale[...] = jnp.broadcast_to(norm[:, 64:65], (C, 128))
    if npatch > 2:
        relay(2)
    grow(nearest(1)).forward()
    grow(band).finish()

    head0 = (idx * own) // HEAD_DIM
    span = nheads * HEAD_DIM
    held = pl.ds(pl.multiple_of(head0 * HEAD_DIM, HEAD_DIM), span)

    def project(source):
        halves = [
            (xr[source, :, k : k + 128].astype(F32) - nmean[...]) * nscale[...]
            for k in range(0, tokens, 128)
        ]
        normed = jnp.concatenate(halves, axis=1).astype(BF16)
        projected = dot(pw[...], normed).astype(BF16)
        wide = projected.astype(F32)
        wide = wide - jnp.mean(wide, axis=0, keepdims=True)
        spread = jnp.mean(wide * wide, axis=0, keepdims=True)
        return projected, (wide * lax.rsqrt(spread + 1e-05)).astype(BF16)

    def score(source, normed):
        keys = dot(kw[held, :], normed).astype(BF16)
        vals[source] = dot(vw[held, :], normed).astype(BF16)
        for h in range(nheads):
            part = slice(h * HEAD_DIM, (h + 1) * HEAD_DIM)
            scores[source, h] = dot_tn(keys[part], query[part])

    projected, normed = project(band)
    proj[...] = projected
    query = (dot(qw[held, :], normed) * 0.125).astype(BF16)
    score(band, normed)

    def arrive(rank):
        source = nearest(rank)
        grow(source).finish()
        score(source, project(source)[1])

    def step(rank):
        relay(rank + 2)
        grow(nearest(rank + 1)).forward()
        arrive(rank)

    loop(1, npatch - 2, step)
    if npatch > 2:
        grow(nearest(npatch - 1)).forward()
        arrive(npatch - 2)
    arrive(npatch - 1)

    for h in range(nheads):
        part = slice(h * HEAD_DIM, (h + 1) * HEAD_DIM)

        def peak_of(b, peak):
            return jnp.maximum(peak, jnp.max(scores[b, h], axis=0, keepdims=True))

        def add(b, so_far):
            total, weighted = so_far
            weights = jnp.exp(scores[b, h] - peak)
            total = total + jnp.sum(weights, axis=0, keepdims=True)
            return total, weighted + dot(vals[b, part], weights.astype(BF16))

        peak = jnp.full((1, tokens), -jnp.inf, F32)
        so_far = (jnp.zeros((1, tokens), F32), jnp.zeros((HEAD_DIM, tokens), F32))
        if npatch <= 4:
            for b in range(npatch):
                peak = peak_of(b, peak)
            for b in range(npatch):
                so_far = add(b, so_far)
        else:
            peak = lax.fori_loop(0, npatch, peak_of, peak)
            so_far = lax.fori_loop(0, npatch, add, so_far)
        attn[part, :] = (so_far[1] / so_far[0]).astype(BF16)

    skip = pl.multiple_of(idx * own - head0 * HEAD_DIM, 16)
    at[mine, :] = attn[pl.ds(skip, own), :]
    gat.start()
    gat.forward()
    gow.finish()
    gat.finish()
    mixed = (proj[...].astype(F32) + dot(ow[...], at[...])).astype(BF16)
    L_PO.wait()
    out[...] = res[...].astype(F32) + dot(po[...], mixed)

    for g in gw + gx + [gpw, gow, gat]:
        g.drain()
    loop(0, npatch, lambda b: grow(b).drain())
    loop(1, npatch, lambda r: zrow(nearest(r), band).wait_send())
    for layer in range(3):
        loop(1, everyone, lambda p: zcopy(layer, p).wait_send())
    for layer in range(2):
        @pl.when(has_below)
        def _():
            hcopy(layer, 0).wait_send()

        @pl.when(has_above)
        def _():
            hcopy(layer, 1).wait_send()


def local(
    npatch, nchan, nsub,
    latent, timestep, time_w1, time_proj, conv1_w, conv2_w, proj_in_w, q_w, kv_w, out_w, proj_out_w,
):
    own, tokens = latent.shape
    nheads = -(-own // HEAD_DIM)
    nidx = nchan * nsub
    temb = time_w1.shape[0]
    half_width = FREQ // 2
    place = lax.broadcasted_iota(jnp.int32, (16, FREQ), 1)
    first = place < half_width
    order = jnp.where(first, place, place - half_width).astype(F32)
    angles = timestep[0].astype(F32) * jnp.exp(-math.log(10000.0) * order / half_width)
    emb = jnp.where(first, jnp.cos(angles), jnp.sin(angles)).astype(BF16)
    vmem = pl.BlockSpec(memory_space=pltpu.VMEM)
    hbm = pl.BlockSpec(memory_space=pl.ANY)
    dma = pltpu.SemaphoreType.DMA
    span = nheads * HEAD_DIM
    ngather = G_LN + npatch
    total = pl.pallas_call(
        functools.partial(kernel, npatch, nchan, nsub, own, nheads),
        out_shape=pltpu.VMEM((own, tokens), F32),
        in_specs=[hbm] * 11,
        out_specs=vmem,
        scratch_shapes=[
            pltpu.VMEM((16, FREQ), BF16),
            pltpu.VMEM((FREQ, temb), BF16),
            pltpu.VMEM((own, temb), BF16),
            pltpu.VMEM((9, own, C), BF16),
            pltpu.VMEM((9, own, C), BF16),
            pltpu.VMEM((own, C), BF16),
        ]
        + [pltpu.VMEM((C, C), BF16)] * 5
        + [pltpu.VMEM((C, tokens), BF16)] * 2
        + [pltpu.VMEM((C, 128), F32)] * 2
        + [
            pltpu.VMEM((C, tokens), BF16),
            pltpu.VMEM((16, own), BF16),
            pltpu.VMEM((own, 16), BF16),
            pltpu.VMEM((C, 3 * nidx * 8), BF16),
        ]
        + [
            pltpu.VMEM((3, npatch, nidx * 8, 128), F32),
            pltpu.VMEM((2, 2, own, tokens), BF16),
            pltpu.VMEM((2, 2, own, tokens), BF16),
            pltpu.VMEM((npatch, C, tokens), BF16),
            pltpu.VMEM((npatch, span, tokens), BF16),
            pltpu.VMEM((npatch, nheads, tokens, tokens), F32),
            pltpu.VMEM((span, tokens), BF16),
            pltpu.VMEM((C, tokens), BF16),
            pltpu.VMEM((own, tokens), BF16),
            dma((12,)),
            dma((ngather, nchan, nsub)),
            dma((ngather, nchan, nsub)),
            dma((3, npatch * nidx)),
            dma((3, npatch * nidx)),
            dma((2, 2)),
            dma((2, 2)),
            dma((npatch,)),
            dma((npatch,)),
        ],
        compiler_params=pltpu.CompilerParams(
            collective_id=0, has_side_effects=True, vmem_limit_bytes=60 * 1024 * 1024
        ),
    )(
        latent, emb, time_w1.T, time_proj, conv1_w, conv2_w, proj_in_w, q_w, kv_w, out_w, proj_out_w
    )
    return total.astype(BF16)


def solution(mesh):
    in_specs = (
        P(("chan", "sub"), ("groups", "patch")),
        P("groups"),
        P(),
        P(("chan", "sub"), None),
        P(None, ("chan", "sub"), None),
        P(None, ("chan", "sub"), None),
        P(("chan", "sub"), None),
        P(("chan", "sub"), None),
        P(None, ("chan", "sub"), None),
        P(("chan", "sub"), None),
        P(("chan", "sub"), None),
    )
    out_specs = P(("chan", "sub"), ("groups", "patch"))
    sizes = [mesh.shape[a] for a in ("patch", "chan", "sub")]
    return jax.shard_map(
        functools.partial(local, *sizes), mesh=mesh, in_specs=in_specs, out_specs=out_specs, check_vma=False
    )
```

```python
import functools
import math

import jax
import jax.numpy as jnp
from jax import lax
from jax.experimental import pallas as pl
from jax.experimental.pallas import tpu as pltpu
from jax.sharding import PartitionSpec as P

C = 640
HEADS = 10
HEAD_DIM = 64
NGROUPS = 32
FREQ = 320
WIDTH = 256
GROUP = C // NGROUPS
MESH = pl.DeviceIdType.MESH
F32 = jnp.float32
BF16 = jnp.bfloat16
HIGH = lax.Precision.HIGHEST

G_PW, G_OW, G_Q, G_K, G_V, G_X1, G_X2, G_AT = range(8)
G_LN = 8


def dot(a, b, precision=None):
    return jnp.dot(a, b, preferred_element_type=F32, precision=precision)


def dot_nt(a, b):
    return lax.dot_general(a, b, (((1,), (1,)), ((), ())), preferred_element_type=F32)


def dot_tn(a, b):
    return lax.dot_general(a, b, (((0,), (0,)), ((), ())), preferred_element_type=F32)


def loop(low, high, body):
    if high - low <= 16:
        for k in range(low, high):
            body(k)
    else:
        lax.fori_loop(low, high, lambda k, _: (body(k), 0)[1], 0)


def silu(v):
    half = 0.5 * v
    return half + half * jnp.tanh(half)


def kernel(
    npatch, nchan, nsub, own, nheads,
    latent_hbm, timestep, time_w1, time_proj, conv1_w, conv2_w, proj_in_w, q_w, kv_w, out_w, proj_out_w,
    out,
    tw1, tpj, cw1, cw2, po, pw, ow, qw, kw, vw, x1, x2, nmean, nscale, at, e16, et16, spread_w, zst, hsend, hrecv,
    xr, vals, scores, peaks, attn, proj, res,
    lsem, gsend, grecv, zsend, zrecv, hssem, hrsem, lnsend, lnrecv,
):
    band = lax.axis_index("patch")
    chan = lax.axis_index("chan")
    sub = lax.axis_index("sub")
    idx = chan * nsub + sub
    nidx = nchan * nsub
    tokens = x1.shape[1]
    aligned = (own * nsub) % HEAD_DIM == 0

    def rows(block, size):
        return pl.ds(pl.multiple_of(block * size, 16 if size % 16 == 0 else 8), size)

    mine = rows(idx, own)
    pairs = [
        (time_w1, tw1), (time_proj, tpj), (q_w, qw.at[mine]), (kv_w.at[0], kw.at[mine]),
        (kv_w.at[1], vw.at[mine]), (proj_in_w, pw.at[mine]), (out_w, ow.at[mine]), (proj_out_w, po),
    ]
    pairs += [(conv1_w, cw1), (conv2_w, cw2), (latent_hbm, x1.at[mine])]
    loads = [pltpu.make_async_copy(a, b, lsem.at[i]) for i, (a, b) in enumerate(pairs)]
    L_T1, L_TP, L_Q, L_K, L_V, L_PW, L_OW, L_PO = loads[:8]
    L_C1, L_C2, L_X = loads[8:]
    for load in (L_X, L_T1, L_TP, L_C1, L_Q, L_K, L_V, L_PW, L_C2, L_OW, L_PO):
        load.start()

    def other(k, by, count):
        to = k + by + count
        to = jnp.where(to >= 2 * count, to - 2 * count, to)
        return jnp.where(to >= count, to - count, to)

    class Gather:
        def __init__(self, g, buf, size, only_sub=False):
            self.g, self.buf, self.size = g, buf, size
            self.chans = 1 if only_sub else nchan

        def copy(self, block, d, s):
            ref = self.buf.at[rows(block, self.size)]
            to = {"chan": other(chan, d, nchan)} if s == 0 else {"sub": other(sub, s, nsub)}
            return pltpu.make_async_remote_copy(
                src_ref=ref, dst_ref=ref, send_sem=gsend.at[self.g, d, s],
                recv_sem=grecv.at[self.g, d, s], device_id=to, device_id_type=MESH,
            )

        def start(self):
            for d in range(1, self.chans):
                self.copy(idx, d, 0).start()
            for s in range(1, nsub):
                self.copy(idx, 0, s).start()

        def forward(self):
            for d in range(1, self.chans):
                block = other(chan, -d, nchan) * nsub + sub
                self.copy(block, d, 0).wait_recv()
                for s in range(1, nsub):
                    self.copy(block, d, s).start()

        def finish(self):
            for d in range(self.chans):
                for s in range(1, nsub):
                    block = other(chan, -d, nchan) * nsub + other(sub, -s, nsub)
                    self.copy(block, d, s).wait_recv()

        def drain(self):
            for d in range(self.chans):
                for s in range(nsub):
                    if d or s:
                        self.copy(idx, d, s).wait_send()

    gw = [
        Gather(G_Q, qw, own, aligned), Gather(G_K, kw, own, aligned), Gather(G_V, vw, own, aligned),
    ]
    gpw, gow = Gather(G_PW, pw, own), Gather(G_OW, ow, own)
    gx = [Gather(G_X1, x1, own), Gather(G_X2, x2, own)]
    gat = Gather(G_AT, at, own)

    cell = GROUP * tokens

    def members(shape, group_dim, size, times=1):
        gi = lax.broadcasted_iota(jnp.int32, shape, group_dim)
        ci = lax.broadcasted_iota(jnp.int32, shape, 1 - group_dim)
        period = shape[group_dim] // times
        for k in range(times - 1, 0, -1):
            gi = jnp.where(gi >= k * period, gi - k * period, gi)
        g = gi & 7
        first = (gi >> 3) * size + g * GROUP
        inside = (ci >= first) & (ci < first + GROUP) & (g < size // GROUP)
        return jnp.where(inside, 1.0, 0.0).astype(BF16)

    def stats(x, layer):
        mean = jnp.sum(dot(e16[...], x), axis=1, keepdims=True) * (1.0 / cell)
        mean = jnp.broadcast_to(mean, (16, 128))
        shift = mean.astype(BF16)
        sc = dot(et16[...], shift)
        sq = jnp.zeros((own, 128), F32)
        for k in range(0, tokens, 128):
            dev = x[:, k : k + 128].astype(F32) - sc
            sq = sq + dev * dev
        hi = sq.astype(BF16)
        lo = (sq - hi.astype(F32)).astype(BF16)
        m2 = jnp.sum(dot(e16[...], jnp.concatenate([hi, lo], axis=1)), axis=1, keepdims=True)
        gap = mean - shift.astype(F32)
        m2 = jnp.maximum(m2 - cell * (gap * gap), 0.0)
        lane = lax.broadcasted_iota(jnp.int32, (16, 128), 1)
        zst[layer, band, rows(idx, 8)] = jnp.where(lane < 64, mean, m2)[0:8]

    everyone = npatch * nidx

    def peer(p, way):
        k = p % nidx
        return {
            "patch": other(band, way * (p // nidx), npatch),
            "chan": other(chan, way * (k // nsub), nchan),
            "sub": other(sub, way * (k % nsub), nsub),
        }

    def zcopy(layer, p, source=None):
        b, k = (band, idx) if source is None else (source["patch"], source["chan"] * nsub + source["sub"])
        ref = zst.at[layer, b, rows(k, 8)]
        return pltpu.make_async_remote_copy(
            src_ref=ref, dst_ref=ref, send_sem=zsend.at[layer, p], recv_sem=zrecv.at[layer, p],
            device_id=peer(p, 1), device_id_type=MESH,
        )

    def share(layer):
        loop(1, everyone, lambda p: zcopy(layer, p).start())

    def combined(layer, eps):
        loop(1, everyone, lambda p: zcopy(layer, p, peer(p, -1)).wait_recv())
        tile = zst[layer]
        means, m2s = tile[:, :, 0:1], tile[:, :, 127:128]
        mean = jnp.sum(means, axis=0) * (1.0 / npatch)
        dev = means - mean[None]
        var = jnp.sum(m2s + cell * (dev * dev), axis=0) * (1.0 / (cell * npatch))
        shape = (nidx * 8, 128)
        lane = lax.broadcasted_iota(jnp.int32, shape, 1)
        pair = jnp.where(
            lane < 64, jnp.broadcast_to(mean, shape), jnp.broadcast_to(lax.rsqrt(var + eps), shape)
        )
        one = pair.astype(BF16)
        rest = pair - one.astype(F32)
        two = rest.astype(BF16)
        three = (rest - two.astype(F32)).astype(BF16)
        return dot(spread_w[...], jnp.concatenate([one, two, three], axis=0))

    def normalize(x, both):
        return (x.astype(F32) - both[:, 0:1]) * both[:, 64:65]

    def hcopy(layer, way):
        return pltpu.make_async_remote_copy(
            src_ref=hsend.at[layer, way], dst_ref=hrecv.at[layer, way],
            send_sem=hssem.at[layer, way], recv_sem=hrsem.at[layer, way],
            device_id={"patch": other(band, 1 - 2 * way, npatch)}, device_id_type=MESH,
        )

    has_above, has_below = band > 0, band < npatch - 1

    def convolve(act, weight, layer):
        col = lax.broadcasted_iota(jnp.int32, act.shape, 1)
        taps = [
            jnp.where(col == 0, 0.0, pltpu.roll(act, 1, 1)).astype(BF16),
            act.astype(BF16),
            jnp.where(col == tokens - 1, 0.0, pltpu.roll(act, tokens - 1, 1)).astype(BF16),
        ]

        def row(i):
            return sum(dot(weight[3 * i + j], taps[j]) for j in range(3))

        hsend[layer, 0] = row(0).astype(BF16)

        @pl.when(has_below)
        def _():
            hcopy(layer, 0).start()

        hsend[layer, 1] = row(2).astype(BF16)

        @pl.when(has_above)
        def _():
            hcopy(layer, 1).start()

        return row(1)

    def neighbours(layer):
        @pl.when(has_above)
        def _():
            hcopy(layer, 0).wait_recv()

        @pl.when(has_below)
        def _():
            hcopy(layer, 1).wait_recv()

        return hrecv[layer, 0].astype(F32) + hrecv[layer, 1].astype(F32)

    for layer in range(2):
        @pl.when(jnp.logical_not(has_above))
        def _():
            hrecv[layer, 0] = jnp.zeros((own, tokens), BF16)

        @pl.when(jnp.logical_not(has_below))
        def _():
            hrecv[layer, 1] = jnp.zeros((own, tokens), BF16)

    barrier = pltpu.get_barrier_semaphore()
    loop(1, everyone, lambda p: pl.semaphore_signal(
        barrier, inc=1, device_id=peer(p, 1), device_id_type=MESH))
    e16[...] = members((16, own), 0, own)
    et16[...] = members((own, 16), 1, own)
    L_X.wait()
    stats(x1[mine, :], 0)
    spread_w[...] = members(spread_w.shape, 1, own, 3)

    half_width = FREQ // 2
    place = lax.broadcasted_iota(jnp.int32, (16, FREQ), 1)
    order = jnp.where(place < half_width, place, place - half_width).astype(F32)
    angles = timestep[0].astype(F32) * jnp.exp(-math.log(10000.0) * order / half_width)
    emb = jnp.where(place < half_width, jnp.cos(angles), jnp.sin(angles)).astype(BF16)
    pl.semaphore_wait(barrier, everyone - 1)

    share(0)
    gx[0].start()
    L_T1.wait()
    hidden = silu(dot(emb, tw1[...]))
    L_TP.wait()
    bias = dot_nt(tpj[...], silu(hidden).astype(BF16))
    gx[0].forward()
    norm = combined(0, 1e-05)
    for load, g in zip((L_Q, L_K, L_V), gw):
        load.wait()
        g.start()
    gx[0].finish()
    L_PW.wait()
    gpw.start()
    L_C1.wait()
    centre = convolve(silu(normalize(x1[...], norm)), cw1, 0)
    conv_one = (centre + neighbours(0) + bias[:, 0:1]).astype(BF16)
    x2[mine, :] = conv_one
    stats(conv_one, 1)

    share(1)
    gx[1].start()
    gpw.forward()
    gx[1].forward()
    norm = combined(1, 1e-05)
    gx[1].finish()
    L_OW.wait()
    gow.start()
    L_C2.wait()
    centre = convolve(silu(normalize(x2[...], norm)), cw2, 1)
    resnet = (x1[mine, :].astype(F32) + (centre + neighbours(1))).astype(BF16)
    res[...] = resnet
    xr[band, mine, :] = resnet

    def zrow(to, source):
        ref = xr.at[source, mine]
        return pltpu.make_async_remote_copy(
            src_ref=ref, dst_ref=ref, send_sem=lnsend.at[to], recv_sem=lnrecv.at[source],
            device_id={"patch": to}, device_id_type=MESH,
        )

    def grow(source):
        return Gather(G_LN + source, xr.at[source], own)

    def nearest(rank):
        near = jnp.minimum(band, npatch - 1 - band)
        odd = rank % 2
        step = (rank + odd) // 2
        beyond = jnp.where(2 * band < npatch - 1, rank, npatch - 1 - rank)
        return jnp.where(rank <= 2 * near, band + (1 - 2 * odd) * step, beyond)

    stats(resnet, 2)
    share(2)
    loop(1, npatch, lambda r: zrow(nearest(r), band).start())
    grow(band).start()
    grow(band).forward()

    def relay(rank):
        source = nearest(rank)
        zrow(source, source).wait_recv()
        grow(source).start()

    gow.forward()
    gpw.finish()
    for g in gw:
        if not aligned:
            g.forward()
        g.finish()
    relay(1)
    norm = combined(2, 1e-06)
    nmean[...] = jnp.broadcast_to(norm[:, 0:1], (C, 128))
    nscale[...] = jnp.broadcast_to(norm[:, 64:65], (C, 128))
    if npatch > 2:
        relay(2)
    grow(nearest(1)).forward()
    grow(band).finish()

    head0 = (idx * own) // HEAD_DIM
    span = nheads * HEAD_DIM
    held = pl.ds(pl.multiple_of(head0 * HEAD_DIM, HEAD_DIM), span)

    def project(source):
        halves = [
            (xr[source, :, k : k + 128].astype(F32) - nmean[...]) * nscale[...]
            for k in range(0, tokens, 128)
        ]
        normed = jnp.concatenate(halves, axis=1).astype(BF16)
        projected = dot(pw[...], normed).astype(BF16)
        wide = projected.astype(F32)
        wide = wide - jnp.mean(wide, axis=0, keepdims=True)
        spread = jnp.mean(wide * wide, axis=0, keepdims=True)
        return projected, (wide * lax.rsqrt(spread + 1e-05)).astype(BF16)

    def score(source, normed):
        keys = dot(kw[held, :], normed).astype(BF16)
        vals[source] = dot(vw[held, :], normed).astype(BF16)
        for h in range(nheads):
            part = slice(h * HEAD_DIM, (h + 1) * HEAD_DIM)
            found = dot_tn(keys[part], query[part])
            scores[source, h] = found
            peaks[source, h] = jnp.max(found, axis=0, keepdims=True)

    projected, normed = project(band)
    proj[...] = projected
    query = (dot(qw[held, :], normed) * 0.125).astype(BF16)
    score(band, normed)

    def arrive(rank):
        source = nearest(rank)
        grow(source).finish()
        score(source, project(source)[1])

    def step(rank):
        relay(rank + 2)
        grow(nearest(rank + 1)).forward()
        arrive(rank)

    loop(1, npatch - 2, step)
    if npatch > 2:
        grow(nearest(npatch - 1)).forward()
        arrive(npatch - 2)
    arrive(npatch - 1)

    for h in range(nheads):
        part = slice(h * HEAD_DIM, (h + 1) * HEAD_DIM)

        def peak_of(b, peak):
            return jnp.maximum(peak, peaks[b, h])

        def add(b, so_far):
            total, weighted = so_far
            weights = jnp.exp(scores[b, h] - peak)
            total = total + jnp.sum(weights, axis=0, keepdims=True)
            return total, weighted + dot(vals[b, part], weights.astype(BF16))

        peak = jnp.full((1, tokens), -jnp.inf, F32)
        so_far = (jnp.zeros((1, tokens), F32), jnp.zeros((HEAD_DIM, tokens), F32))
        if npatch <= 4:
            for b in range(npatch):
                peak = peak_of(b, peak)
            for b in range(npatch):
                so_far = add(b, so_far)
        else:
            peak = lax.fori_loop(0, npatch, peak_of, peak)
            so_far = lax.fori_loop(0, npatch, add, so_far)
        attn[part, :] = (so_far[1] / so_far[0]).astype(BF16)

    skip = pl.multiple_of(idx * own - head0 * HEAD_DIM, 16)
    at[mine, :] = attn[pl.ds(skip, own), :]
    gat.start()
    gat.forward()
    gow.finish()
    gat.finish()
    mixed = (proj[...].astype(F32) + dot(ow[...], at[...])).astype(BF16)
    L_PO.wait()
    out[...] = res[...].astype(F32) + dot(po[...], mixed)

    for g in gw + gx + [gpw, gow, gat]:
        g.drain()
    loop(0, npatch, lambda b: grow(b).drain())
    loop(1, npatch, lambda r: zrow(nearest(r), band).wait_send())
    for layer in range(3):
        loop(1, everyone, lambda p: zcopy(layer, p).wait_send())
    for layer in range(2):
        @pl.when(has_below)
        def _():
            hcopy(layer, 0).wait_send()

        @pl.when(has_above)
        def _():
            hcopy(layer, 1).wait_send()


def local(
    npatch, nchan, nsub,
    latent, timestep, time_w1, time_proj, conv1_w, conv2_w, proj_in_w, q_w, kv_w, out_w, proj_out_w,
):
    own, tokens = latent.shape
    nheads = -(-own // HEAD_DIM)
    nidx = nchan * nsub
    temb = time_w1.shape[0]
    vmem = pl.BlockSpec(memory_space=pltpu.VMEM)
    hbm = pl.BlockSpec(memory_space=pl.ANY)
    dma = pltpu.SemaphoreType.DMA
    span = nheads * HEAD_DIM
    ngather = G_LN + npatch
    total = pl.pallas_call(
        functools.partial(kernel, npatch, nchan, nsub, own, nheads),
        out_shape=pltpu.VMEM((own, tokens), F32),
        in_specs=[hbm, pl.BlockSpec(memory_space=pltpu.SMEM)] + [hbm] * 9,
        out_specs=vmem,
        scratch_shapes=[
            pltpu.VMEM((FREQ, temb), BF16),
            pltpu.VMEM((own, temb), BF16),
            pltpu.VMEM((9, own, C), BF16),
            pltpu.VMEM((9, own, C), BF16),
            pltpu.VMEM((own, C), BF16),
        ]
        + [pltpu.VMEM((C, C), BF16)] * 5
        + [pltpu.VMEM((C, tokens), BF16)] * 2
        + [pltpu.VMEM((C, 128), F32)] * 2
        + [
            pltpu.VMEM((C, tokens), BF16),
            pltpu.VMEM((16, own), BF16),
            pltpu.VMEM((own, 16), BF16),
            pltpu.VMEM((C, 3 * nidx * 8), BF16),
        ]
        + [
            pltpu.VMEM((3, npatch, nidx * 8, 128), F32),
            pltpu.VMEM((2, 2, own, tokens), BF16),
            pltpu.VMEM((2, 2, own, tokens), BF16),
            pltpu.VMEM((npatch, C, tokens), BF16),
            pltpu.VMEM((npatch, span, tokens), BF16),
            pltpu.VMEM((npatch, nheads, tokens, tokens), F32),
            pltpu.VMEM((npatch, nheads, 1, tokens), F32),
            pltpu.VMEM((span, tokens), BF16),
            pltpu.VMEM((C, tokens), BF16),
            pltpu.VMEM((own, tokens), BF16),
            dma((11,)),
            dma((ngather, nchan, nsub)),
            dma((ngather, nchan, nsub)),
            dma((3, npatch * nidx)),
            dma((3, npatch * nidx)),
            dma((2, 2)),
            dma((2, 2)),
            dma((npatch,)),
            dma((npatch,)),
        ],
        compiler_params=pltpu.CompilerParams(
            collective_id=0, has_side_effects=True, vmem_limit_bytes=60 * 1024 * 1024
        ),
    )(
        latent, timestep, time_w1.T, time_proj, conv1_w, conv2_w, proj_in_w, q_w, kv_w, out_w, proj_out_w
    )
    return total.astype(BF16)


def solution(mesh):
    in_specs = (
        P(("chan", "sub"), ("groups", "patch")),
        P("groups"),
        P(),
        P(("chan", "sub"), None),
        P(None, ("chan", "sub"), None),
        P(None, ("chan", "sub"), None),
        P(("chan", "sub"), None),
        P(("chan", "sub"), None),
        P(None, ("chan", "sub"), None),
        P(("chan", "sub"), None),
        P(("chan", "sub"), None),
    )
    out_specs = P(("chan", "sub"), ("groups", "patch"))
    sizes = [mesh.shape[a] for a in ("patch", "chan", "sub")]
    return jax.shard_map(
        functools.partial(local, *sizes), mesh=mesh, in_specs=in_specs, out_specs=out_specs, check_vma=False
    )
```

```python
import functools
import math

import jax
import jax.numpy as jnp
from jax import lax
from jax.experimental import pallas as pl
from jax.experimental.pallas import tpu as pltpu
from jax.sharding import PartitionSpec as P

C = 640
HEADS = 10
HEAD_DIM = 64
NGROUPS = 32
FREQ = 320
WIDTH = 256
GROUP = C // NGROUPS
MESH = pl.DeviceIdType.MESH
F32 = jnp.float32
BF16 = jnp.bfloat16
HIGH = lax.Precision.HIGHEST

G_PW, G_OW, G_Q, G_K, G_V, G_X1, G_X2, G_AT = range(8)
G_LN = 8


def dot(a, b, precision=None):
    return jnp.dot(a, b, preferred_element_type=F32, precision=precision)


def dot_nt(a, b):
    return lax.dot_general(a, b, (((1,), (1,)), ((), ())), preferred_element_type=F32)


def dot_tn(a, b):
    return lax.dot_general(a, b, (((0,), (0,)), ((), ())), preferred_element_type=F32)


def loop(low, high, body):
    if high - low <= 16:
        for k in range(low, high):
            body(k)
    else:
        lax.fori_loop(low, high, lambda k, _: (body(k), 0)[1], 0)


def silu(v):
    half = 0.5 * v
    return half + half * jnp.tanh(half)


def kernel(
    npatch, nchan, nsub, own, nheads,
    latent_hbm, timestep, time_w1, time_proj, conv1_w, conv2_w, proj_in_w, q_w, kv_w, out_w, proj_out_w,
    out,
    tw1, tpj, cw1, cw2, po, pw, ow, qw, kw, vw, x1, x2, nmean, nscale, at, e16, et16, spread_w, zst, hsend, hrecv,
    xr, vals, scores, peaks, attn, proj, res,
    lsem, gsend, grecv, zsend, zrecv, hssem, hrsem, lnsend, lnrecv,
):
    band = lax.axis_index("patch")
    chan = lax.axis_index("chan")
    sub = lax.axis_index("sub")
    idx = chan * nsub + sub
    nidx = nchan * nsub
    tokens = x1.shape[1]
    aligned = (own * nsub) % HEAD_DIM == 0

    def rows(block, size):
        return pl.ds(pl.multiple_of(block * size, 16 if size % 16 == 0 else 8), size)

    mine = rows(idx, own)
    pairs = [
        (time_w1, tw1), (time_proj, tpj), (q_w, qw.at[mine]), (kv_w.at[0], kw.at[mine]),
        (kv_w.at[1], vw.at[mine]), (proj_in_w, pw.at[mine]), (out_w, ow.at[mine]), (proj_out_w, po),
    ]
    pairs += [(conv1_w, cw1), (conv2_w, cw2), (latent_hbm, x1.at[mine])]
    loads = [pltpu.make_async_copy(a, b, lsem.at[i]) for i, (a, b) in enumerate(pairs)]
    L_T1, L_TP, L_Q, L_K, L_V, L_PW, L_OW, L_PO = loads[:8]
    L_C1, L_C2, L_X = loads[8:]
    for load in (L_X, L_T1, L_TP, L_C1, L_Q, L_K, L_V, L_PW, L_C2, L_OW, L_PO):
        load.start()

    def other(k, by, count):
        to = k + by + count
        to = jnp.where(to >= 2 * count, to - 2 * count, to)
        return jnp.where(to >= count, to - count, to)

    class Gather:
        def __init__(self, g, buf, size, only_sub=False):
            self.g, self.buf, self.size = g, buf, size
            self.chans = 1 if only_sub else nchan

        def copy(self, block, d, s):
            ref = self.buf.at[rows(block, self.size)]
            to = {"chan": other(chan, d, nchan)} if s == 0 else {"sub": other(sub, s, nsub)}
            return pltpu.make_async_remote_copy(
                src_ref=ref, dst_ref=ref, send_sem=gsend.at[self.g, d, s],
                recv_sem=grecv.at[self.g, d, s], device_id=to, device_id_type=MESH,
            )

        def start(self):
            for d in range(1, self.chans):
                self.copy(idx, d, 0).start()
            for s in range(1, nsub):
                self.copy(idx, 0, s).start()

        def forward(self):
            for d in range(1, self.chans):
                block = other(chan, -d, nchan) * nsub + sub
                self.copy(block, d, 0).wait_recv()
                for s in range(1, nsub):
                    self.copy(block, d, s).start()

        def finish(self):
            for d in range(self.chans):
                for s in range(1, nsub):
                    block = other(chan, -d, nchan) * nsub + other(sub, -s, nsub)
                    self.copy(block, d, s).wait_recv()

        def drain(self):
            for d in range(self.chans):
                for s in range(nsub):
                    if d or s:
                        self.copy(idx, d, s).wait_send()

    gw = [
        Gather(G_Q, qw, own, aligned), Gather(G_K, kw, own, aligned), Gather(G_V, vw, own, aligned),
    ]
    gpw, gow = Gather(G_PW, pw, own), Gather(G_OW, ow, own)
    gx = [Gather(G_X1, x1, own), Gather(G_X2, x2, own)]
    gat = Gather(G_AT, at, own)

    cell = GROUP * tokens

    def members(shape, group_dim, size, times=1):
        gi = lax.broadcasted_iota(jnp.int32, shape, group_dim)
        ci = lax.broadcasted_iota(jnp.int32, shape, 1 - group_dim)
        period = shape[group_dim] // times
        for k in range(times - 1, 0, -1):
            gi = jnp.where(gi >= k * period, gi - k * period, gi)
        g = gi & 7
        first = (gi >> 3) * size + g * GROUP
        inside = (ci >= first) & (ci < first + GROUP) & (g < size // GROUP)
        return jnp.where(inside, 1.0, 0.0).astype(BF16)

    def stats(x, layer):
        mean = jnp.sum(dot(e16[...], x), axis=1, keepdims=True) * (1.0 / cell)
        mean = jnp.broadcast_to(mean, (16, 128))
        shift = mean.astype(BF16)
        sc = dot(et16[...], shift)
        sq = jnp.zeros((own, 128), F32)
        for k in range(0, tokens, 128):
            dev = x[:, k : k + 128].astype(F32) - sc
            sq = sq + dev * dev
        hi = sq.astype(BF16)
        lo = (sq - hi.astype(F32)).astype(BF16)
        m2 = jnp.sum(dot(e16[...], jnp.concatenate([hi, lo], axis=1)), axis=1, keepdims=True)
        gap = mean - shift.astype(F32)
        m2 = jnp.maximum(m2 - cell * (gap * gap), 0.0)
        lane = lax.broadcasted_iota(jnp.int32, (16, 128), 1)
        zst[layer, band, rows(idx, 8)] = jnp.where(lane < 64, mean, m2)[0:8]

    everyone = npatch * nidx

    def peer(p, way):
        k = p % nidx
        return {
            "patch": other(band, way * (p // nidx), npatch),
            "chan": other(chan, way * (k // nsub), nchan),
            "sub": other(sub, way * (k % nsub), nsub),
        }

    def zcopy(layer, p, source=None):
        b, k = (band, idx) if source is None else (source["patch"], source["chan"] * nsub + source["sub"])
        ref = zst.at[layer, b, rows(k, 8)]
        return pltpu.make_async_remote_copy(
            src_ref=ref, dst_ref=ref, send_sem=zsend.at[layer, p], recv_sem=zrecv.at[layer, p],
            device_id=peer(p, 1), device_id_type=MESH,
        )

    def share(layer):
        loop(1, everyone, lambda p: zcopy(layer, p).start())

    def combined(layer, eps):
        loop(1, everyone, lambda p: zcopy(layer, p, peer(p, -1)).wait_recv())
        tile = zst[layer]
        means, m2s = tile[:, :, 0:1], tile[:, :, 127:128]
        mean = jnp.sum(means, axis=0) * (1.0 / npatch)
        dev = means - mean[None]
        var = jnp.sum(m2s + cell * (dev * dev), axis=0) * (1.0 / (cell * npatch))
        shape = (nidx * 8, 128)
        lane = lax.broadcasted_iota(jnp.int32, shape, 1)
        pair = jnp.where(
            lane < 64, jnp.broadcast_to(mean, shape), jnp.broadcast_to(lax.rsqrt(var + eps), shape)
        )
        one = pair.astype(BF16)
        rest = pair - one.astype(F32)
        two = rest.astype(BF16)
        three = (rest - two.astype(F32)).astype(BF16)
        return dot(spread_w[...], jnp.concatenate([one, two, three], axis=0))

    def normalize(x, both):
        return (x.astype(F32) - both[:, 0:1]) * both[:, 64:65]

    def hcopy(layer, way):
        return pltpu.make_async_remote_copy(
            src_ref=hsend.at[layer, way], dst_ref=hrecv.at[layer, way],
            send_sem=hssem.at[layer, way], recv_sem=hrsem.at[layer, way],
            device_id={"patch": other(band, 1 - 2 * way, npatch)}, device_id_type=MESH,
        )

    has_above, has_below = band > 0, band < npatch - 1

    def convolve(act, weight, layer):
        col = lax.broadcasted_iota(jnp.int32, act.shape, 1)
        taps = [
            jnp.where(col == 0, 0.0, pltpu.roll(act, 1, 1)).astype(BF16),
            act.astype(BF16),
            jnp.where(col == tokens - 1, 0.0, pltpu.roll(act, tokens - 1, 1)).astype(BF16),
        ]

        def row(i):
            return sum(dot(weight[3 * i + j], taps[j]) for j in range(3))

        hsend[layer, 0] = row(0).astype(BF16)

        @pl.when(has_below)
        def _():
            hcopy(layer, 0).start()

        hsend[layer, 1] = row(2).astype(BF16)

        @pl.when(has_above)
        def _():
            hcopy(layer, 1).start()

        return row(1)

    def neighbours(layer):
        @pl.when(has_above)
        def _():
            hcopy(layer, 0).wait_recv()

        @pl.when(has_below)
        def _():
            hcopy(layer, 1).wait_recv()

        return hrecv[layer, 0].astype(F32) + hrecv[layer, 1].astype(F32)

    for layer in range(2):
        @pl.when(jnp.logical_not(has_above))
        def _():
            hrecv[layer, 0] = jnp.zeros((own, tokens), BF16)

        @pl.when(jnp.logical_not(has_below))
        def _():
            hrecv[layer, 1] = jnp.zeros((own, tokens), BF16)

    barrier = pltpu.get_barrier_semaphore()
    loop(1, everyone, lambda p: pl.semaphore_signal(
        barrier, inc=1, device_id=peer(p, 1), device_id_type=MESH))
    e16[...] = members((16, own), 0, own)
    et16[...] = members((own, 16), 1, own)
    L_X.wait()
    stats(x1[mine, :], 0)
    spread_w[...] = members(spread_w.shape, 1, own, 3)

    half_width = FREQ // 2
    place = lax.broadcasted_iota(jnp.int32, (16, FREQ), 1)
    order = jnp.where(place < half_width, place, place - half_width).astype(F32)
    angles = timestep[0].astype(F32) * jnp.exp(-math.log(10000.0) * order / half_width)
    emb = jnp.where(place < half_width, jnp.cos(angles), jnp.sin(angles)).astype(BF16)
    pl.semaphore_wait(barrier, everyone - 1)

    share(0)
    gx[0].start()
    L_T1.wait()
    hidden = silu(dot(emb, tw1[...]))
    L_TP.wait()
    bias = dot_nt(tpj[...], silu(hidden).astype(BF16))
    gx[0].forward()
    norm = combined(0, 1e-05)
    for load, g in zip((L_Q, L_K, L_V), gw):
        load.wait()
        g.start()
    gx[0].finish()
    L_PW.wait()
    gpw.start()
    L_C1.wait()
    centre = convolve(silu(normalize(x1[...], norm)), cw1, 0)
    conv_one = (centre + neighbours(0) + bias[:, 0:1]).astype(BF16)
    x2[mine, :] = conv_one
    stats(conv_one, 1)

    share(1)
    gx[1].start()
    gpw.forward()
    gx[1].forward()
    norm = combined(1, 1e-05)
    gx[1].finish()
    L_OW.wait()
    gow.start()
    L_C2.wait()
    centre = convolve(silu(normalize(x2[...], norm)), cw2, 1)
    resnet = (x1[mine, :].astype(F32) + (centre + neighbours(1))).astype(BF16)
    res[...] = resnet
    xr[band, mine, :] = resnet

    def zrow(to, source):
        ref = xr.at[source, mine]
        return pltpu.make_async_remote_copy(
            src_ref=ref, dst_ref=ref, send_sem=lnsend.at[to], recv_sem=lnrecv.at[source],
            device_id={"patch": to}, device_id_type=MESH,
        )

    def grow(source):
        return Gather(G_LN + source, xr.at[source], own)

    def nearest(rank):
        near = jnp.minimum(band, npatch - 1 - band)
        odd = rank % 2
        step = (rank + odd) // 2
        beyond = jnp.where(2 * band < npatch - 1, rank, npatch - 1 - rank)
        return jnp.where(rank <= 2 * near, band + (1 - 2 * odd) * step, beyond)

    stats(resnet, 2)
    share(2)
    loop(1, npatch, lambda r: zrow(nearest(npatch - r), band).start())
    grow(band).start()
    grow(band).forward()

    def relay(rank):
        source = nearest(rank)
        zrow(source, source).wait_recv()
        grow(source).start()

    gow.forward()
    gpw.finish()
    for g in gw:
        if not aligned:
            g.forward()
        g.finish()
    relay(1)
    norm = combined(2, 1e-06)
    nmean[...] = jnp.broadcast_to(norm[:, 0:1], (C, 128))
    nscale[...] = jnp.broadcast_to(norm[:, 64:65], (C, 128))
    if npatch > 2:
        relay(2)
    grow(nearest(1)).forward()
    grow(band).finish()

    head0 = (idx * own) // HEAD_DIM
    span = nheads * HEAD_DIM
    held = pl.ds(pl.multiple_of(head0 * HEAD_DIM, HEAD_DIM), span)

    def project(source):
        halves = [
            (xr[source, :, k : k + 128].astype(F32) - nmean[...]) * nscale[...]
            for k in range(0, tokens, 128)
        ]
        normed = jnp.concatenate(halves, axis=1).astype(BF16)
        projected = dot(pw[...], normed).astype(BF16)
        wide = projected.astype(F32)
        wide = wide - jnp.mean(wide, axis=0, keepdims=True)
        spread = jnp.mean(wide * wide, axis=0, keepdims=True)
        return projected, (wide * lax.rsqrt(spread + 1e-05)).astype(BF16)

    def score(source, normed):
        keys = dot(kw[held, :], normed).astype(BF16)
        vals[source] = dot(vw[held, :], normed).astype(BF16)
        for h in range(nheads):
            part = slice(h * HEAD_DIM, (h + 1) * HEAD_DIM)
            found = dot_tn(keys[part], query[part])
            scores[source, h] = found
            peaks[source, h] = jnp.max(found, axis=0, keepdims=True)

    projected, normed = project(band)
    proj[...] = projected
    query = (dot(qw[held, :], normed) * 0.125).astype(BF16)
    score(band, normed)

    def arrive(rank):
        source = nearest(rank)
        grow(source).finish()
        score(source, project(source)[1])

    def step(rank):
        relay(rank + 2)
        grow(nearest(rank + 1)).forward()
        arrive(rank)

    loop(1, npatch - 2, step)
    if npatch > 2:
        grow(nearest(npatch - 1)).forward()
        arrive(npatch - 2)
    arrive(npatch - 1)

    for h in range(nheads):
        part = slice(h * HEAD_DIM, (h + 1) * HEAD_DIM)

        def peak_of(b, peak):
            return jnp.maximum(peak, peaks[b, h])

        def add(b, so_far):
            total, weighted = so_far
            weights = jnp.exp(scores[b, h] - peak)
            total = total + jnp.sum(weights, axis=0, keepdims=True)
            return total, weighted + dot(vals[b, part], weights.astype(BF16))

        peak = jnp.full((1, tokens), -jnp.inf, F32)
        so_far = (jnp.zeros((1, tokens), F32), jnp.zeros((HEAD_DIM, tokens), F32))
        if npatch <= 4:
            for b in range(npatch):
                peak = peak_of(b, peak)
            for b in range(npatch):
                so_far = add(b, so_far)
        else:
            peak = lax.fori_loop(0, npatch, peak_of, peak)
            so_far = lax.fori_loop(0, npatch, add, so_far)
        attn[part, :] = (so_far[1] / so_far[0]).astype(BF16)

    skip = pl.multiple_of(idx * own - head0 * HEAD_DIM, 16)
    at[mine, :] = attn[pl.ds(skip, own), :]
    gat.start()
    gat.forward()
    gow.finish()
    gat.finish()
    mixed = (proj[...].astype(F32) + dot(ow[...], at[...])).astype(BF16)
    L_PO.wait()
    out[...] = res[...].astype(F32) + dot(po[...], mixed)

    for g in gw + gx + [gpw, gow, gat]:
        g.drain()
    loop(0, npatch, lambda b: grow(b).drain())
    loop(1, npatch, lambda r: zrow(nearest(r), band).wait_send())
    for layer in range(3):
        loop(1, everyone, lambda p: zcopy(layer, p).wait_send())
    for layer in range(2):
        @pl.when(has_below)
        def _():
            hcopy(layer, 0).wait_send()

        @pl.when(has_above)
        def _():
            hcopy(layer, 1).wait_send()


def local(
    npatch, nchan, nsub,
    latent, timestep, time_w1, time_proj, conv1_w, conv2_w, proj_in_w, q_w, kv_w, out_w, proj_out_w,
):
    own, tokens = latent.shape
    nheads = -(-own // HEAD_DIM)
    nidx = nchan * nsub
    temb = time_w1.shape[0]
    vmem = pl.BlockSpec(memory_space=pltpu.VMEM)
    hbm = pl.BlockSpec(memory_space=pl.ANY)
    dma = pltpu.SemaphoreType.DMA
    span = nheads * HEAD_DIM
    ngather = G_LN + npatch
    total = pl.pallas_call(
        functools.partial(kernel, npatch, nchan, nsub, own, nheads),
        out_shape=pltpu.VMEM((own, tokens), F32),
        in_specs=[hbm, pl.BlockSpec(memory_space=pltpu.SMEM)] + [hbm] * 9,
        out_specs=vmem,
        scratch_shapes=[
            pltpu.VMEM((FREQ, temb), BF16),
            pltpu.VMEM((own, temb), BF16),
            pltpu.VMEM((9, own, C), BF16),
            pltpu.VMEM((9, own, C), BF16),
            pltpu.VMEM((own, C), BF16),
        ]
        + [pltpu.VMEM((C, C), BF16)] * 5
        + [pltpu.VMEM((C, tokens), BF16)] * 2
        + [pltpu.VMEM((C, 128), F32)] * 2
        + [
            pltpu.VMEM((C, tokens), BF16),
            pltpu.VMEM((16, own), BF16),
            pltpu.VMEM((own, 16), BF16),
            pltpu.VMEM((C, 3 * nidx * 8), BF16),
        ]
        + [
            pltpu.VMEM((3, npatch, nidx * 8, 128), F32),
            pltpu.VMEM((2, 2, own, tokens), BF16),
            pltpu.VMEM((2, 2, own, tokens), BF16),
            pltpu.VMEM((npatch, C, tokens), BF16),
            pltpu.VMEM((npatch, span, tokens), BF16),
            pltpu.VMEM((npatch, nheads, tokens, tokens), F32),
            pltpu.VMEM((npatch, nheads, 1, tokens), F32),
            pltpu.VMEM((span, tokens), BF16),
            pltpu.VMEM((C, tokens), BF16),
            pltpu.VMEM((own, tokens), BF16),
            dma((11,)),
            dma((ngather, nchan, nsub)),
            dma((ngather, nchan, nsub)),
            dma((3, npatch * nidx)),
            dma((3, npatch * nidx)),
            dma((2, 2)),
            dma((2, 2)),
            dma((npatch,)),
            dma((npatch,)),
        ],
        compiler_params=pltpu.CompilerParams(
            collective_id=0, has_side_effects=True, vmem_limit_bytes=60 * 1024 * 1024
        ),
    )(
        latent, timestep, time_w1.T, time_proj, conv1_w, conv2_w, proj_in_w, q_w, kv_w, out_w, proj_out_w
    )
    return total.astype(BF16)


def solution(mesh):
    in_specs = (
        P(("chan", "sub"), ("groups", "patch")),
        P("groups"),
        P(),
        P(("chan", "sub"), None),
        P(None, ("chan", "sub"), None),
        P(None, ("chan", "sub"), None),
        P(("chan", "sub"), None),
        P(("chan", "sub"), None),
        P(None, ("chan", "sub"), None),
        P(("chan", "sub"), None),
        P(("chan", "sub"), None),
    )
    out_specs = P(("chan", "sub"), ("groups", "patch"))
    sizes = [mesh.shape[a] for a in ("patch", "chan", "sub")]
    return jax.shard_map(
        functools.partial(local, *sizes), mesh=mesh, in_specs=in_specs, out_specs=out_specs, check_vma=False
    )
```
